32 devices in a mesh: rep: 4 (over y, core), fsdp: 8 (over z, x).
Axes of the slice: x: 2, y: 2, z: 4, core: 2. Of those that a mesh axis runs over, the one named last changes fastest.
Arguments:
- tokens: bfloat16 [32768, 8192], P(('rep', 'fsdp')), may hold values from -6 to 6
- cotangent: bfloat16 [32768, 512], P(('rep', 'fsdp')), may hold values from -0.03125 to 0.03125
- old_weight: bfloat16 [8192, 512], P(('rep', 'fsdp')), may hold values from -0.0625 to 0.0625
- old_first: float32 [8192, 512], P(('rep', 'fsdp')), may hold values from -4 to 4
- old_second: float32 [8192, 512], P(('rep', 'fsdp')), may hold values from 0.05 to 2
- old_owner: int32 [32], replicated, may hold values from 0 to 31, each once
- new_owner: int32 [8], replicated, may hold values from 0 to 7, each once
Outputs:
- projected: bfloat16 [32768, 512], P(('rep', 'fsdp'))
- new_weight: bfloat16 [8192, 512], P(('rep', 'fsdp'))
- new_first: float32 [8192, 512], P(('rep', 'fsdp'))
- new_second: float32 [8192, 512], P(('rep', 'fsdp'))
The draws below stay inside these ranges and needn't reach their ends.
Inputs may be any that keep to these rules, and one draw needn't show every extreme that they name: `old_owner`: a permutation. `new_owner`: a permutation.
All inputs are finite; a program needn't handle non-finite values.
Results may differ from the reference program's by a relative error of at most 0.008.
Values may be sent and summed in bfloat16 or wider, within the bound.
No kernel may reach another device: no remote copies, remote signals or barrier semaphores. Data moves between devices by JAX's collectives and lax.ppermute only.
A program may use at most 192 MiB of HBM per device.

```python
import math
import jax
import jax.numpy as jnp
from jax import lax

D = 8192
KV = 512
TOKENS = 32768
N_REP = 4
N_FSDP = 8
DEVICES = 32


def spiked(entries, stream_key, source, target, shards_of, factor):
    owner, partner = [(jnp.arange(entries.shape[dim]) // (entries.shape[dim] // shards_of)).reshape([-1 if axis == dim else 1 for axis in range(entries.ndim)]) for dim in (source, target)]
    chosen = jax.random.permutation(stream_key, shards_of)[partner]
    strong = (owner == chosen) | (owner == (partner + shards_of // 2) % shards_of)
    return jnp.where(strong, factor * entries, entries)


def steps_of(rng, dims, split, least, largest):
    def one(position, shards_of):
        steps = jax.random.uniform(jax.random.fold_in(jax.random.fold_in(rng, 6), position), (shards_of,), jnp.float32, least / len(split), largest / len(split))
        return jnp.repeat(jnp.exp(steps), dims[position] // shards_of).reshape((-1,) + (1,) * (len(dims) - position - 1))

    gain = one(*split[0])
    for cut in split[1:]:
        gain = gain * one(*cut)
    return gain


def bell_draw(rng, dims, deviation, most, pieces=(), kind=jnp.bfloat16):
    factor_of = steps_of(rng, dims, pieces, -0.22, 0.18) if pieces else 1.0
    values = jax.random.normal(rng, dims, jnp.float32) * deviation * factor_of
    return jnp.minimum(jnp.maximum(values, -most), most).astype(kind)


def gaussian_with(stream_key, dims, scale, limit, shards, heavy, kind=jnp.bfloat16):
    result = scale * jax.random.normal(stream_key, dims, jnp.float32)
    if shards:
        result = result * steps_of(stream_key, dims, shards, -0.22, 0.18)
    return jnp.clip(spiked(result, jax.random.fold_in(stream_key, 3), *heavy), -limit, limit).astype(kind)


def setup_inputs(seed: int = 0) -> dict:
    streams_of = jax.random.split(jax.random.key(seed), 8)
    tokens = gaussian_with(streams_of[0], (TOKENS, D), 1.0, 6.0, ((0, 32),), (0, 1, 32, 2.75))
    cotangent = bell_draw(streams_of[1], (TOKENS, KV), TOKENS ** -0.5, 0.03125, ((0, 32),))
    old_weight = bell_draw(streams_of[2], (D, KV), D ** -0.5, 0.0625, ((0, 32),))
    old_first = bell_draw(streams_of[3], (D, KV), 0.5, 4.0, ((0, 32),), jnp.float32)
    old_second = jnp.clip(jnp.exp(math.log(2.0) - 3.6888794 * jax.random.uniform(streams_of[4], (D, KV), jnp.float32) ** steps_of(streams_of[4], (D, KV), ((0, 32),), -0.2, 0.2)), 0.05, 2.0)
    old_owner = jax.random.permutation(streams_of[5], DEVICES).astype(jnp.int32)
    new_owner = jax.random.permutation(streams_of[6], N_FSDP).astype(jnp.int32)
    return dict(tokens=tokens, cotangent=cotangent, old_weight=old_weight, old_first=old_first, old_second=old_second, old_owner=old_owner, new_owner=new_owner)


beta_one = 0.9
beta_two = 0.95
learn_rate = 0.001
decay_rate = 0.1
epsilon = 1e-08
correction_one = 1.0 - 0.9 ** 10
correction_two = 1.0 - 0.95 ** 10

def reference(tokens, cotangent, old_weight, old_first, old_second, old_owner, new_owner):
    row_block = D // DEVICES
    strip = D * KV // (DEVICES * DEVICES)
    slot_ids = jnp.arange(DEVICES, dtype=jnp.int32)
    inverse = jnp.zeros((DEVICES,), jnp.int32).at[old_owner.astype(jnp.int32)].set(slot_ids)
    placing = jnp.take(new_owner.astype(jnp.int32), slot_ids % N_FSDP) * N_REP + slot_ids // N_FSDP

    def logical(source):
        held = jnp.take(source.reshape(DEVICES, DEVICES, strip), inverse, axis=0)
        return jnp.transpose(held, (1, 0, 2)).reshape(D, KV)

    def placed(source):
        return jnp.take(source.reshape(DEVICES, row_block, KV), placing, axis=0).reshape(D, KV)
    weight = logical(old_weight)
    moment_one = logical(old_first)
    moment_two = logical(old_second)
    projected = jnp.dot(tokens, weight, preferred_element_type=jnp.float32).astype(jnp.bfloat16)
    gradient = lax.dot_general(tokens, cotangent, (((0,), (0,)), ((), ())), preferred_element_type=jnp.float32)
    first_next = beta_one * moment_one + (1.0 - beta_one) * gradient
    second_next = beta_two * moment_two + (1.0 - beta_two) * gradient * gradient
    step_size = first_next / correction_one / (jnp.sqrt(second_next / correction_two) + epsilon)
    updated = (weight.astype(jnp.float32) * (1.0 - learn_rate * decay_rate) - learn_rate * step_size).astype(jnp.bfloat16)
    return (projected, placed(updated), placed(first_next), placed(second_next))
```

```python
import functools
import jax
import jax.numpy as jnp
from jax import lax
from jax.experimental import pallas as pl
from jax.experimental.pallas import tpu as pltpu
from jax.sharding import PartitionSpec as P

beta_one = 0.9
beta_two = 0.95
learn_rate = 0.001
decay_rate = 0.1
epsilon = 1e-08
correction_one = 1.0 - 0.9**10
correction_two = 1.0 - 0.95**10

AXES = ("rep", "fsdp")
GRANT = 48 * 1024 * 1024
SUB = 8
PER_STEP = 4


def cost(flops, moved):
    return pl.CostEstimate(flops=flops, bytes_accessed=moved, transcendentals=0)


def grad_kernel(order_ref, *refs):
    token_refs, (cot_ref, out_ref, turned) = refs[:-3], refs[-3:]

    @pl.when(pl.program_id(0) == 0)
    def _():
        turned[...] = cot_ref[...].T

    for slot, token_ref in enumerate(token_refs):
        out_ref[slot] = jnp.dot(
            turned[...], token_ref[...], preferred_element_type=jnp.float32
        ).astype(out_ref.dtype)


def grad_blocks(tokens, cotangent, order, row_block):
    rows, features = tokens.shape
    width = cotangent.shape[1]
    blocks = order.shape[0]
    if row_block % 128 or blocks % PER_STEP:
        whole = lax.dot_general(
            cotangent, tokens, (((0,), (0,)), ((), ())), preferred_element_type=jnp.float32
        ).astype(jnp.bfloat16)
        cut = jnp.transpose(whole.reshape(width, features // row_block, row_block), (1, 0, 2))
        return jnp.take(cut, order, axis=0)

    def token_map(slot):
        return lambda i, order_ref: (0, order_ref[i * PER_STEP + slot])

    return pl.pallas_call(
        grad_kernel,
        grid_spec=pltpu.PrefetchScalarGridSpec(
            num_scalar_prefetch=1,
            grid=(blocks // PER_STEP,),
            in_specs=[pl.BlockSpec((rows, row_block), token_map(s)) for s in range(PER_STEP)]
            + [pl.BlockSpec((rows, width), lambda i, order_ref: (0, 0))],
            out_specs=pl.BlockSpec((PER_STEP, width, row_block), lambda i, order_ref: (i, 0, 0)),
            scratch_shapes=[pltpu.VMEM((width, rows), jnp.bfloat16)],
        ),
        out_shape=jax.ShapeDtypeStruct((blocks, width, row_block), jnp.bfloat16),
        compiler_params=pltpu.CompilerParams(vmem_limit_bytes=GRANT),
        cost_estimate=cost(
            2 * rows * width * blocks * row_block,
            2 * blocks * row_block * (rows + width) + 2 * rows * width,
        ),
        name="weight_gradient",
    )(order, *([tokens] * PER_STEP), cotangent)


def pack_kernel(placing_ref, first_ref, second_ref, out_ref):
    for slot in range(out_ref.shape[0]):
        rows = pl.ds(pl.multiple_of(placing_ref[slot] * SUB, SUB), SUB)
        pair = jnp.concatenate([first_ref[rows, :], second_ref[rows, :]], axis=0)
        out_ref[slot] = pair.astype(out_ref.dtype)


def pack_moments(first, second, placing):
    devices = placing.shape[0]
    width = first.shape[1]
    return pl.pallas_call(
        pack_kernel,
        in_specs=[
            pl.BlockSpec(memory_space=pltpu.SMEM),
            pl.BlockSpec(memory_space=pltpu.VMEM),
            pl.BlockSpec(memory_space=pltpu.VMEM),
        ],
        out_specs=pl.BlockSpec(memory_space=pltpu.VMEM),
        out_shape=jax.ShapeDtypeStruct((devices, 2 * SUB, width), jnp.bfloat16),
        cost_estimate=cost(0, 12 * first.size),
        name="pack_moments",
    )(placing, first, second)


def project_kernel(inverse_ref, own_ref, token_ref, held_ref, out_ref, rows_ref, logical):
    devices, row_block, _ = held_ref.shape

    @pl.when(pl.program_id(0) == 0)
    def _():
        def place(pair, carry):
            even = inverse_ref[2 * pair]
            odd = inverse_ref[2 * pair + 1]
            for block in range(0, devices, 2):
                span = pl.ds(block * SUB, 2 * SUB)
                top = held_ref[even, span, :]
                low = held_ref[odd, span, :]
                for half in range(2):
                    part = slice(half * SUB, (half + 1) * SUB)
                    start = (block + half) * row_block + pair * 2 * SUB
                    logical[pl.ds(pl.multiple_of(start, 2 * SUB), 2 * SUB), :] = jnp.concatenate(
                        [top[part], low[part]], axis=0
                    )
            return carry

        lax.fori_loop(0, devices // 2, place, 0)
        start = pl.multiple_of(own_ref[0] * row_block, row_block)
        rows_ref[...] = logical[pl.ds(start, row_block), :]

    out_ref[...] = jnp.dot(
        token_ref[...], logical[...], preferred_element_type=jnp.float32
    ).astype(out_ref.dtype)


def project(tokens, held, inverse, own):
    rows, features = tokens.shape
    devices, row_block, width = held.shape
    tile = rows // 4
    return pl.pallas_call(
        project_kernel,
        grid_spec=pltpu.PrefetchScalarGridSpec(
            num_scalar_prefetch=2,
            grid=(rows // tile,),
            in_specs=[
                pl.BlockSpec((tile, features), lambda i, *_: (i, 0)),
                pl.BlockSpec((devices, row_block, width), lambda i, *_: (0, 0, 0)),
            ],
            out_specs=[
                pl.BlockSpec((tile, width), lambda i, *_: (i, 0)),
                pl.BlockSpec((row_block, width), lambda i, *_: (0, 0)),
            ],
            scratch_shapes=[pltpu.VMEM((features, width), jnp.bfloat16)],
        ),
        out_shape=[
            jax.ShapeDtypeStruct((rows, width), jnp.bfloat16),
            jax.ShapeDtypeStruct((row_block, width), jnp.bfloat16),
        ],
        compiler_params=pltpu.CompilerParams(vmem_limit_bytes=GRANT),
        cost_estimate=cost(
            2 * rows * width * features, 2 * (rows * features + features * width + rows * width)
        ),
        name="project",
    )(inverse, own, tokens, held)


def adam(weight_rows, first_rows, second_rows, gradient):
    first_next = beta_one * first_rows + (1.0 - beta_one) * gradient
    second_next = beta_two * second_rows + (1.0 - beta_two) * gradient * gradient
    step_size = first_next / correction_one / (jnp.sqrt(second_next / correction_two) + epsilon)
    updated = (
        weight_rows.astype(jnp.float32) * (1.0 - learn_rate * decay_rate) - learn_rate * step_size
    ).astype(jnp.bfloat16)
    return updated, first_next, second_next


def adam_kernel(
    inverse_ref, turned_ref, moments_ref, weight_ref, new_ref, first_ref, second_ref, gradient
):
    gradient[...] = turned_ref[...].astype(jnp.float32).T
    for pair in range(moments_ref.shape[0] // 2):
        even = moments_ref[inverse_ref[2 * pair]].astype(jnp.float32)
        odd = moments_ref[inverse_ref[2 * pair + 1]].astype(jnp.float32)
        rows = pl.ds(pair * 2 * SUB, 2 * SUB)
        new_ref[rows, :], first_ref[rows, :], second_ref[rows, :] = adam(
            weight_ref[rows, :],
            jnp.concatenate([even[:SUB], odd[:SUB]], axis=0),
            jnp.concatenate([even[SUB:], odd[SUB:]], axis=0),
            gradient[rows, :],
        )


def adam_rows(turned, moments, weight_rows, inverse):
    row_block, width = weight_rows.shape
    return pl.pallas_call(
        adam_kernel,
        in_specs=[pl.BlockSpec(memory_space=pltpu.SMEM)]
        + [pl.BlockSpec(memory_space=pltpu.VMEM)] * 3,
        out_specs=[pl.BlockSpec(memory_space=pltpu.VMEM)] * 3,
        out_shape=[
            jax.ShapeDtypeStruct((row_block, width), jnp.bfloat16),
            jax.ShapeDtypeStruct((row_block, width), jnp.float32),
            jax.ShapeDtypeStruct((row_block, width), jnp.float32),
        ],
        scratch_shapes=[pltpu.VMEM((row_block, width), jnp.float32)],
        compiler_params=pltpu.CompilerParams(vmem_limit_bytes=GRANT),
        cost_estimate=cost(20 * row_block * width, 16 * row_block * width),
        name="adam_rows",
    )(inverse, turned, moments, weight_rows)


def body(tokens, cotangent, old_weight, old_first, old_second, old_owner, new_owner):
    devices = lax.axis_size(AXES)
    groups = lax.axis_size("rep")
    shards = lax.axis_size("fsdp")
    features = tokens.shape[1]
    row_block, width = old_weight.shape
    strip = row_block * width // devices
    slot_ids = jnp.arange(devices, dtype=jnp.int32)
    placing = jnp.take(new_owner, slot_ids % shards) * groups + slot_ids // shards
    inverse = jnp.zeros((devices,), jnp.int32).at[old_owner].set(slot_ids)
    own_block = jnp.take(placing, lax.axis_index(AXES))
    by_tile = row_block == devices * SUB and width % 128 == 0 and devices % 2 == 0

    held = lax.all_gather(old_weight, AXES, axis=0, tiled=False)
    if by_tile:
        packed = pack_moments(old_first, old_second, placing)
    else:
        both = jnp.stack([old_first, old_second]).astype(jnp.bfloat16)
        packed = jnp.take(
            jnp.transpose(both.reshape(2, devices, strip), (1, 0, 2)), placing, axis=0
        )
    arrived = lax.all_to_all(packed, AXES, split_axis=0, concat_axis=0, tiled=True)

    partial = grad_blocks(tokens, cotangent, placing, row_block)
    turned = lax.psum_scatter(partial, AXES, scatter_dimension=0, tiled=True).reshape(
        width, row_block
    )
    if by_tile:
        projected, weight_rows = project(tokens, held, inverse, own_block.reshape(1))
        return (projected, *adam_rows(turned, arrived, weight_rows, inverse))
    logical = jnp.transpose(
        jnp.take(held.reshape(devices, devices, strip), inverse, axis=0), (1, 0, 2)
    ).reshape(features, width)
    projected = jnp.dot(tokens, logical, preferred_element_type=jnp.float32).astype(jnp.bfloat16)
    weight_rows = lax.dynamic_slice_in_dim(logical, own_block * row_block, row_block, 0)
    moved = jnp.transpose(jnp.take(arrived, inverse, axis=0), (1, 0, 2))
    first_rows, second_rows = moved.astype(jnp.float32).reshape(2, row_block, width)
    return (projected, *adam(weight_rows, first_rows, second_rows, turned.T.astype(jnp.float32)))


def solution(mesh):
    placed = P(AXES, None)
    return jax.shard_map(
        body,
        mesh=mesh,
        in_specs=(placed,) * 5 + (P(), P()),
        out_specs=(placed,) * 4,
        check_vma=False,
    )
```

```python
import functools
import jax
import jax.numpy as jnp
from jax import lax
from jax.experimental import pallas as pl
from jax.experimental.pallas import tpu as pltpu
from jax.sharding import PartitionSpec as P

beta_one = 0.9
beta_two = 0.95
learn_rate = 0.001
decay_rate = 0.1
epsilon = 1e-08
correction_one = 1.0 - 0.9**10
correction_two = 1.0 - 0.95**10

AXES = ("rep", "fsdp")
GRANT = 48 * 1024 * 1024
SUB = 8


def cost(flops, moved):
    return pl.CostEstimate(flops=flops, bytes_accessed=moved, transcendentals=0)


def grad_kernel(order_ref, *refs):
    per_step = order_ref.shape[0] // pl.num_programs(0)
    token_refs, turned_ref, out_refs = refs[:per_step], refs[per_step], refs[per_step + 1 :]
    for step, out_ref in enumerate(out_refs):

        @pl.when(pl.program_id(0) == step)
        def _():
            for slot, token_ref in enumerate(token_refs):
                out_ref[slot] = jnp.dot(
                    turned_ref[...], token_ref[...], preferred_element_type=jnp.float32
                ).astype(out_ref.dtype)


def grad_blocks(tokens, turned, order, row_block, parts):
    rows, features = tokens.shape
    width = turned.shape[0]
    per_step = order.shape[0] // parts
    if row_block % 128:
        whole = jnp.dot(turned, tokens, preferred_element_type=jnp.float32).astype(jnp.bfloat16)
        cut = jnp.transpose(whole.reshape(width, features // row_block, row_block), (1, 0, 2))
        return [jnp.take(cut, part, axis=0) for part in order.reshape(parts, per_step)]

    def token_map(slot):
        return lambda i, order_ref: (0, order_ref[i * per_step + slot])

    block = (per_step, width, row_block)
    return pl.pallas_call(
        grad_kernel,
        grid_spec=pltpu.PrefetchScalarGridSpec(
            num_scalar_prefetch=1,
            grid=(parts,),
            in_specs=[pl.BlockSpec((rows, row_block), token_map(s)) for s in range(per_step)]
            + [pl.BlockSpec((width, rows), lambda i, order_ref: (0, 0))],
            out_specs=[pl.BlockSpec(block, lambda i, order_ref: (0, 0, 0))] * parts,
        ),
        out_shape=[jax.ShapeDtypeStruct(block, jnp.bfloat16)] * parts,
        compiler_params=pltpu.CompilerParams(vmem_limit_bytes=GRANT),
        cost_estimate=cost(
            2 * rows * width * order.shape[0] * row_block,
            2 * order.shape[0] * row_block * (rows + width) + 2 * rows * width,
        ),
        name="weight_gradient",
    )(order, *([tokens] * per_step), turned)


def pack_kernel(placing_ref, first_ref, second_ref, out_ref):
    for slot in range(out_ref.shape[0]):
        rows = pl.ds(pl.multiple_of(placing_ref[slot] * SUB, SUB), SUB)
        pair = jnp.concatenate([first_ref[rows, :], second_ref[rows, :]], axis=0)
        out_ref[slot] = pair.astype(out_ref.dtype)


def pack_moments(first, second, placing):
    devices = placing.shape[0]
    width = first.shape[1]
    return pl.pallas_call(
        pack_kernel,
        in_specs=[
            pl.BlockSpec(memory_space=pltpu.SMEM),
            pl.BlockSpec(memory_space=pltpu.VMEM),
            pl.BlockSpec(memory_space=pltpu.VMEM),
        ],
        out_specs=pl.BlockSpec(memory_space=pltpu.VMEM),
        out_shape=jax.ShapeDtypeStruct((devices, 2 * SUB, width), jnp.bfloat16),
        cost_estimate=cost(0, 12 * first.size),
        name="pack_moments",
    )(placing, first, second)


def project_kernel(counts, owner_ref, own_ref, token_ref, *refs):
    piece_refs = refs[: len(counts)]
    out_ref, rows_ref, held, logical, sems = refs[len(counts) :]
    devices, row_block, _ = held.shape

    @pl.when(pl.program_id(0) == 0)
    def _():
        copies = []
        for piece_ref, count in zip(piece_refs, counts):
            for index in range(count):
                slot = len(copies)
                copies.append(
                    pltpu.make_async_copy(
                        piece_ref.at[index], held.at[owner_ref[slot]], sems.at[slot]
                    )
                )
        for copy in copies:
            copy.start()
        for copy in copies:
            copy.wait()

        def place(pair, carry):
            for block in range(0, devices, 2):
                span = pl.ds(block * SUB, 2 * SUB)
                top = held[2 * pair, span, :]
                low = held[2 * pair + 1, span, :]
                for half in range(2):
                    part = slice(half * SUB, (half + 1) * SUB)
                    start = (block + half) * row_block + pair * 2 * SUB
                    logical[pl.ds(pl.multiple_of(start, 2 * SUB), 2 * SUB), :] = jnp.concatenate(
                        [top[part], low[part]], axis=0
                    )
            return carry

        lax.fori_loop(0, devices // 2, place, 0)
        start = pl.multiple_of(own_ref[0] * row_block, row_block)
        rows_ref[...] = logical[pl.ds(start, row_block), :]

    out_ref[...] = jnp.dot(
        token_ref[...], logical[...], preferred_element_type=jnp.float32
    ).astype(out_ref.dtype)


def project(tokens, pieces, owners, own):
    rows, features = tokens.shape
    _, row_block, width = pieces[0].shape
    devices = owners.shape[0]
    counts = tuple(piece.shape[0] for piece in pieces)
    tile = rows // 4
    return pl.pallas_call(
        functools.partial(project_kernel, counts),
        grid_spec=pltpu.PrefetchScalarGridSpec(
            num_scalar_prefetch=2,
            grid=(rows // tile,),
            in_specs=[pl.BlockSpec((tile, features), lambda i, *_: (i, 0))]
            + [pl.BlockSpec(memory_space=pl.ANY)] * len(pieces),
            out_specs=[
                pl.BlockSpec((tile, width), lambda i, *_: (i, 0)),
                pl.BlockSpec((row_block, width), lambda i, *_: (0, 0)),
            ],
            scratch_shapes=[
                pltpu.VMEM((devices, row_block, width), jnp.bfloat16),
                pltpu.VMEM((features, width), jnp.bfloat16),
                pltpu.SemaphoreType.DMA((devices,)),
            ],
        ),
        out_shape=[
            jax.ShapeDtypeStruct((rows, width), jnp.bfloat16),
            jax.ShapeDtypeStruct((row_block, width), jnp.bfloat16),
        ],
        compiler_params=pltpu.CompilerParams(vmem_limit_bytes=GRANT),
        cost_estimate=cost(
            2 * rows * width * features, 2 * (rows * features + features * width + rows * width)
        ),
        name="project",
    )(owners, own, tokens, *pieces)


def adam(weight_rows, first_rows, second_rows, gradient):
    first_next = beta_one * first_rows + (1.0 - beta_one) * gradient
    second_next = beta_two * second_rows + (1.0 - beta_two) * gradient * gradient
    step_size = first_next / correction_one / (jnp.sqrt(second_next / correction_two) + epsilon)
    updated = (
        weight_rows.astype(jnp.float32) * (1.0 - learn_rate * decay_rate) - learn_rate * step_size
    ).astype(jnp.bfloat16)
    return updated, first_next, second_next


def adam_kernel(inverse_ref, moments_ref, weight_ref, *refs):
    part_refs, (new_ref, first_ref, second_ref, gradient) = refs[:-4], refs[-4:]
    total = part_refs[0][0].astype(jnp.float32)
    for part_ref in part_refs[1:]:
        total = total + part_ref[0].astype(jnp.float32)
    gradient[...] = total.T
    for pair in range(moments_ref.shape[0] // 2):
        even = moments_ref[inverse_ref[2 * pair]].astype(jnp.float32)
        odd = moments_ref[inverse_ref[2 * pair + 1]].astype(jnp.float32)
        rows = pl.ds(pair * 2 * SUB, 2 * SUB)
        new_ref[rows, :], first_ref[rows, :], second_ref[rows, :] = adam(
            weight_ref[rows, :],
            jnp.concatenate([even[:SUB], odd[:SUB]], axis=0),
            jnp.concatenate([even[SUB:], odd[SUB:]], axis=0),
            gradient[rows, :],
        )


def adam_rows(parts, moments, weight_rows, inverse):
    row_block, width = weight_rows.shape
    whole = pl.BlockSpec((row_block, width), lambda i, *_: (0, 0))
    return pl.pallas_call(
        adam_kernel,
        grid_spec=pltpu.PrefetchScalarGridSpec(
            num_scalar_prefetch=1,
            grid=(1,),
            in_specs=[pl.BlockSpec(moments.shape, lambda i, *_: (0, 0, 0)), whole]
            + [pl.BlockSpec((1, width, row_block), lambda i, *_: (0, 0, 0))] * len(parts),
            out_specs=[whole] * 3,
            scratch_shapes=[pltpu.VMEM((row_block, width), jnp.float32)],
        ),
        out_shape=[
            jax.ShapeDtypeStruct((row_block, width), jnp.bfloat16),
            jax.ShapeDtypeStruct((row_block, width), jnp.float32),
            jax.ShapeDtypeStruct((row_block, width), jnp.float32),
        ],
        compiler_params=pltpu.CompilerParams(vmem_limit_bytes=GRANT),
        cost_estimate=cost(20 * row_block * width, 16 * row_block * width),
        name="adam_rows",
    )(inverse, moments, weight_rows, *parts)


class Grid:
    def __init__(self, groups, shards):
        self.shards = shards
        self.cores = 2 if groups % 2 == 0 else 1
        self.minor = 2 if shards % 2 == 0 else 1
        self.outer = groups // self.cores
        self.far = shards // self.minor
        self.swaps = self.cores == 2 and self.minor == self.outer
        self.near, self.side = self.minor, self.outer

    def moved(self, position, core=0, near=0, side=0, far=0):
        group, shard = position // self.shards, position % self.shards
        outer, on = group // self.cores, (group % self.cores + core) % self.cores
        depth, minor = shard // self.minor, shard % self.minor
        swapped = on if self.swaps else 0
        minor = (minor + near + (side - near) * swapped) % self.minor
        outer = (outer + side + (near - side) * swapped) % self.outer
        depth = (depth + far) % self.far
        return (outer * self.cores + on) * self.shards + depth * self.minor + minor

    def send(self, value, **steps):
        devices = self.outer * self.cores * self.shards
        pairs = [(p, self.moved(p, **steps)) for p in range(devices)]
        return lax.ppermute(value, AXES, pairs)


def rounded_sum(*terms):
    total = terms[0].astype(jnp.float32)
    for term in terms[1:]:
        total = total + term.astype(jnp.float32)
    return total.astype(terms[0].dtype)


def reduce_rows(grid, blocks_of):
    near, side = grid.near, grid.side
    last = []
    for far in sorted(range(grid.far), key=lambda k: -min(k, grid.far - k)):
        parts = blocks_of(far)
        terms = [parts[0]]
        for core in range(1, grid.cores):
            terms.append(grid.send(parts[core], core=core))
        kept = list(terms)
        for step in range(1, near):
            cut = slice(step * side, (step + 1) * side)
            kept.append(grid.send(rounded_sum(*[t[cut] for t in terms]), near=step))
        ends = list(kept)
        for step in range(1, side):
            cut = slice(step, step + 1)
            ends.append(grid.send(rounded_sum(*[t[cut] for t in kept]), side=step))
        if far:
            last.append(grid.send(rounded_sum(*[t[:1] for t in ends]), far=far))
        else:
            last.extend(ends)
    return last


def body(tokens, cotangent, old_weight, old_first, old_second, old_owner, new_owner):
    devices = lax.axis_size(AXES)
    groups = lax.axis_size("rep")
    shards = lax.axis_size("fsdp")
    features = tokens.shape[1]
    row_block, width = old_weight.shape
    strip = row_block * width // devices
    grid = Grid(groups, shards)
    me = lax.axis_index(AXES)
    slot_ids = jnp.arange(devices, dtype=jnp.int32)
    placing = jnp.take(new_owner, slot_ids % shards) * groups + slot_ids // shards
    inverse = jnp.zeros((devices,), jnp.int32).at[old_owner].set(slot_ids)
    own_block = jnp.take(placing, me)
    by_tile = row_block == devices * SUB and width % 128 == 0 and devices % 2 == 0

    held = lax.all_gather(old_weight, AXES, axis=0, tiled=False)
    if by_tile:
        packed = pack_moments(old_first, old_second, placing)
    else:
        both = jnp.stack([old_first, old_second]).astype(jnp.bfloat16)
        packed = jnp.take(
            jnp.transpose(both.reshape(2, devices, strip), (1, 0, 2)), placing, axis=0
        )
    arrived = lax.all_to_all(packed, AXES, split_axis=0, concat_axis=0, tiled=True)

    cot_turned = cotangent.T

    def blocks_of(far):
        targets = [
            grid.moved(me, core, near, side, far)
            for core in reversed(range(grid.cores))
            for near in range(grid.near)
            for side in range(grid.side)
        ]
        order = jnp.take(placing, jnp.stack(targets))
        return grad_blocks(tokens, cot_turned, order, row_block, grid.cores)[::-1]

    parts = reduce_rows(grid, blocks_of)
    if by_tile:
        projected, weight_rows = project(tokens, [held], old_owner, own_block.reshape(1))
        return (projected, *adam_rows(parts, arrived, weight_rows, inverse))
    logical = jnp.transpose(
        jnp.take(held.reshape(devices, devices, strip), inverse, axis=0), (1, 0, 2)
    ).reshape(features, width)
    projected = jnp.dot(tokens, logical, preferred_element_type=jnp.float32).astype(jnp.bfloat16)
    weight_rows = lax.dynamic_slice_in_dim(logical, own_block * row_block, row_block, 0)
    moved = jnp.transpose(jnp.take(arrived, inverse, axis=0), (1, 0, 2))
    first_rows, second_rows = moved.astype(jnp.float32).reshape(2, row_block, width)
    gradient = sum(part[0].astype(jnp.float32) for part in parts).T
    return (projected, *adam(weight_rows, first_rows, second_rows, gradient))


def solution(mesh):
    placed = P(AXES, None)
    return jax.shard_map(
        body,
        mesh=mesh,
        in_specs=(placed,) * 5 + (P(), P()),
        out_specs=(placed,) * 4,
        check_vma=False,
    )
```

```python
import functools
import jax
import jax.numpy as jnp
import numpy as np
from jax import lax
from jax.experimental import pallas as pl
from jax.experimental.pallas import tpu as pltpu
from jax.sharding import PartitionSpec as P

beta_one = 0.9
beta_two = 0.95
learn_rate = 0.001
decay_rate = 0.1
epsilon = 1e-08
correction_one = 1.0 - 0.9**10
correction_two = 1.0 - 0.95**10

AXES = ("rep", "fsdp")
GRANT = 48 * 1024 * 1024
SUB = 8


def cost(flops, moved):
    return pl.CostEstimate(flops=flops, bytes_accessed=moved, transcendentals=0)


def grad_kernel(per_step, adds, order_ref, *refs):
    token_refs, turned_ref, refs = refs[:per_step], refs[per_step], refs[per_step + 1 :]
    out_refs = refs[adds:]

    def write(out_ref):
        for slot, token_ref in enumerate(token_refs):
            block = jnp.dot(turned_ref[...], token_ref[...], preferred_element_type=jnp.float32)
            if adds:
                block = block + refs[0][slot].astype(jnp.float32)
            out_ref[slot] = block.astype(out_ref.dtype)

    if len(out_refs) == 1:
        write(out_refs[0])
        return
    for step, out_ref in enumerate(out_refs):
        pl.when(pl.program_id(0) == step)(functools.partial(write, out_ref))


def grad_blocks(tokens, turned, order, first, steps, per_step, row_block, addend=None, cut=False):
    rows, features = tokens.shape
    width = turned.shape[0]
    blocks = steps * per_step
    if row_block % 128:
        whole = jnp.dot(turned, tokens, preferred_element_type=jnp.float32)
        parts = jnp.transpose(whole.reshape(width, features // row_block, row_block), (1, 0, 2))
        parts = jnp.take(parts, order[first : first + blocks], axis=0)
        if addend is not None:
            parts = parts + addend.astype(jnp.float32)
        parts = parts.astype(jnp.bfloat16)
        return list(jnp.split(parts, steps)) if cut else [parts]

    def token_map(slot):
        return lambda i, order_ref: (0, order_ref[first + i * per_step + slot])

    block = pl.BlockSpec((per_step, width, row_block), lambda i, order_ref: (i, 0, 0))
    fixed = pl.BlockSpec((per_step, width, row_block), lambda i, order_ref: (0, 0, 0))
    added = [] if addend is None else [addend]
    outs = steps if cut else 1
    return pl.pallas_call(
        functools.partial(grad_kernel, per_step, len(added)),
        grid_spec=pltpu.PrefetchScalarGridSpec(
            num_scalar_prefetch=1,
            grid=(steps,),
            in_specs=[pl.BlockSpec((rows, row_block), token_map(s)) for s in range(per_step)]
            + [pl.BlockSpec((width, rows), lambda i, order_ref: (0, 0))]
            + [block] * len(added),
            out_specs=[fixed if cut else block] * outs,
        ),
        out_shape=[jax.ShapeDtypeStruct((blocks // outs, width, row_block), jnp.bfloat16)] * outs,
        compiler_params=pltpu.CompilerParams(vmem_limit_bytes=GRANT),
        cost_estimate=cost(
            2 * rows * width * blocks * row_block,
            2 * blocks * row_block * (rows + width * (1 + len(added))) + 2 * rows * width,
        ),
        name="weight_gradient",
    )(order, *([tokens] * per_step), turned, *added)


def pack_kernel(groups, new_ref, first_ref, second_ref, out_ref):
    shards = new_ref.shape[0]
    for slot in range(out_ref.shape[0]):
        block = new_ref[slot % shards] * groups + slot // shards
        rows = pl.ds(pl.multiple_of(block * SUB, SUB), SUB)
        pair = jnp.concatenate([first_ref[rows, :], second_ref[rows, :]], axis=0)
        out_ref[slot] = pair.astype(out_ref.dtype)


def pack_moments(first, second, new_owner, groups):
    devices = new_owner.shape[0] * groups
    width = first.shape[1]
    return pl.pallas_call(
        functools.partial(pack_kernel, groups),
        in_specs=[
            pl.BlockSpec(memory_space=pltpu.SMEM),
            pl.BlockSpec(memory_space=pltpu.VMEM),
            pl.BlockSpec(memory_space=pltpu.VMEM),
        ],
        out_specs=pl.BlockSpec(memory_space=pltpu.VMEM),
        out_shape=jax.ShapeDtypeStruct((devices, 2 * SUB, width), jnp.bfloat16),
        cost_estimate=cost(0, 12 * first.size),
        name="pack_moments",
    )(new_owner, first, second)


def project_kernel(counts, owner_ref, order_ref, token_ref, *refs):
    piece_refs = refs[: len(counts)]
    out_ref, rows_ref, held, logical, sems = refs[len(counts) :]
    devices, row_block, _ = held.shape

    @pl.when(pl.program_id(0) == 0)
    def _():
        copies = []
        start = 0
        for piece_ref, count in zip(piece_refs, counts):
            for slot in range(devices):
                target = held.at[owner_ref[slot], pl.ds(start, count)]
                copies.append(
                    pltpu.make_async_copy(piece_ref.at[slot], target, sems.at[len(copies)])
                )
            start += count
        for copy in copies:
            copy.start()
        for copy in copies:
            copy.wait()

        def place(pair, carry):
            for block in range(0, devices, 2):
                span = pl.ds(block * SUB, 2 * SUB)
                top = held[2 * pair, span, :]
                low = held[2 * pair + 1, span, :]
                for half in range(2):
                    part = slice(half * SUB, (half + 1) * SUB)
                    start = (block + half) * row_block + pair * 2 * SUB
                    logical[pl.ds(pl.multiple_of(start, 2 * SUB), 2 * SUB), :] = jnp.concatenate(
                        [top[part], low[part]], axis=0
                    )
            return carry

        lax.fori_loop(0, devices // 2, place, 0)
        start = pl.multiple_of(order_ref[0] * row_block, row_block)
        rows_ref[...] = logical[pl.ds(start, row_block), :]

    out_ref[...] = jnp.dot(
        token_ref[...], logical[...], preferred_element_type=jnp.float32
    ).astype(out_ref.dtype)


def project(tokens, pieces, owners, order):
    rows, features = tokens.shape
    devices, _, width = pieces[0].shape
    counts = tuple(piece.shape[1] for piece in pieces)
    row_block = sum(counts)
    tile = rows // 4
    return pl.pallas_call(
        functools.partial(project_kernel, counts),
        grid_spec=pltpu.PrefetchScalarGridSpec(
            num_scalar_prefetch=2,
            grid=(rows // tile,),
            in_specs=[pl.BlockSpec((tile, features), lambda i, *_: (i, 0))]
            + [pl.BlockSpec(memory_space=pl.ANY)] * len(pieces),
            out_specs=[
                pl.BlockSpec((tile, width), lambda i, *_: (i, 0)),
                pl.BlockSpec((row_block, width), lambda i, *_: (0, 0)),
            ],
            scratch_shapes=[
                pltpu.VMEM((devices, row_block, width), jnp.bfloat16),
                pltpu.VMEM((features, width), jnp.bfloat16),
                pltpu.SemaphoreType.DMA((devices * len(pieces),)),
            ],
        ),
        out_shape=[
            jax.ShapeDtypeStruct((rows, width), jnp.bfloat16),
            jax.ShapeDtypeStruct((row_block, width), jnp.bfloat16),
        ],
        compiler_params=pltpu.CompilerParams(vmem_limit_bytes=GRANT),
        cost_estimate=cost(
            2 * rows * width * features, 2 * (rows * features + features * width + rows * width)
        ),
        name="project",
    )(owners, order, tokens, *pieces)


def adam(weight_rows, first_rows, second_rows, gradient):
    first_next = beta_one * first_rows + (1.0 - beta_one) * gradient
    second_next = beta_two * second_rows + (1.0 - beta_two) * gradient * gradient
    step_size = first_next / correction_one / (jnp.sqrt(second_next / correction_two) + epsilon)
    updated = (
        weight_rows.astype(jnp.float32) * (1.0 - learn_rate * decay_rate) - learn_rate * step_size
    ).astype(jnp.bfloat16)
    return updated, first_next, second_next


def adam_kernel(owner_ref, moments_ref, weight_ref, *refs):
    part_refs, (new_ref, first_ref, second_ref, gradient, inverse_ref) = refs[:-5], refs[-5:]
    for slot in range(moments_ref.shape[0]):
        inverse_ref[owner_ref[slot]] = slot
    total = part_refs[0][0].astype(jnp.float32)
    for part_ref in part_refs[1:]:
        total = total + part_ref[0].astype(jnp.float32)
    gradient[...] = total.T
    for pair in range(moments_ref.shape[0] // 2):
        even = moments_ref[inverse_ref[2 * pair]].astype(jnp.float32)
        odd = moments_ref[inverse_ref[2 * pair + 1]].astype(jnp.float32)
        rows = pl.ds(pair * 2 * SUB, 2 * SUB)
        new_ref[rows, :], first_ref[rows, :], second_ref[rows, :] = adam(
            weight_ref[rows, :],
            jnp.concatenate([even[:SUB], odd[:SUB]], axis=0),
            jnp.concatenate([even[SUB:], odd[SUB:]], axis=0),
            gradient[rows, :],
        )


def adam_rows(parts, moments, weight_rows, owners):
    row_block, width = weight_rows.shape
    whole = pl.BlockSpec((row_block, width), lambda i, *_: (0, 0))
    return pl.pallas_call(
        adam_kernel,
        grid_spec=pltpu.PrefetchScalarGridSpec(
            num_scalar_prefetch=1,
            grid=(1,),
            in_specs=[pl.BlockSpec(moments.shape, lambda i, *_: (0, 0, 0)), whole]
            + [pl.BlockSpec((1, width, row_block), lambda i, *_: (0, 0, 0))] * len(parts),
            out_specs=[whole] * 3,
            scratch_shapes=[
                pltpu.VMEM((row_block, width), jnp.float32),
                pltpu.SMEM((moments.shape[0],), jnp.int32),
            ],
        ),
        out_shape=[
            jax.ShapeDtypeStruct((row_block, width), jnp.bfloat16),
            jax.ShapeDtypeStruct((row_block, width), jnp.float32),
            jax.ShapeDtypeStruct((row_block, width), jnp.float32),
        ],
        compiler_params=pltpu.CompilerParams(vmem_limit_bytes=GRANT),
        cost_estimate=cost(20 * row_block * width, 16 * row_block * width),
        name="adam_rows",
    )(owners, moments, weight_rows, *parts)


class Grid:
    def __init__(self, groups, shards):
        self.shards = shards
        self.cores = 2 if groups % 2 == 0 else 1
        self.minor = 2 if shards % 2 == 0 else 1
        self.outer = groups // self.cores
        self.far = shards // self.minor
        self.swaps = self.cores == 2 and self.minor == self.outer
        self.near, self.side = self.minor, self.outer

    def moved(self, position, core=0, near=0, side=0, far=0):
        group, shard = position // self.shards, position % self.shards
        outer, on = group // self.cores, (group % self.cores + core) % self.cores
        depth, minor = shard // self.minor, shard % self.minor
        swapped = on if self.swaps else 0
        minor = (minor + near + (side - near) * swapped) % self.minor
        outer = (outer + side + (near - side) * swapped) % self.outer
        depth = (depth + far) % self.far
        return (outer * self.cores + on) * self.shards + depth * self.minor + minor

    def send(self, value, **steps):
        devices = self.outer * self.cores * self.shards
        pairs = [(p, self.moved(p, **steps)) for p in range(devices)]
        return lax.ppermute(value, AXES, pairs)


def rounded_sum(*terms):
    total = terms[0].astype(jnp.float32)
    for term in terms[1:]:
        total = total + term.astype(jnp.float32)
    return total.astype(terms[0].dtype)


def far_first(grid):
    return sorted(range(grid.far), key=lambda k: -min(k, grid.far - k))


def order_table(grid):
    steps = [
        dict(core=core, near=near, side=side, far=far)
        for far in range(grid.far)
        for core in range(grid.cores)
        for near in [*range(1, grid.near), 0]
        for side in range(grid.side)
    ]
    return np.array([[grid.moved(p, **step) for step in steps] for p in range(len(steps))], np.int32)


def reduce_rows(grid, blocks_of):
    last = []
    for far in far_first(grid):
        addend = None
        if grid.cores > 1:
            addend = grid.send(blocks_of(1, far, None, False)[0], core=1)
        parts = blocks_of(0, far, addend, True)
        kept = [parts[-1]]
        for step, part in enumerate(parts[:-1], 1):
            kept.append(grid.send(part, near=step))
        ends = list(kept)
        for step in range(1, grid.side):
            cut = slice(step, step + 1)
            ends.append(grid.send(rounded_sum(*[t[cut] for t in kept]), side=step))
        if far:
            last.append(grid.send(rounded_sum(*[t[:1] for t in ends]), far=far))
        else:
            last.extend(ends)
    return last


def body(tokens, cotangent, old_weight, old_first, old_second, old_owner, new_owner):
    devices = lax.axis_size(AXES)
    groups = lax.axis_size("rep")
    shards = lax.axis_size("fsdp")
    features = tokens.shape[1]
    row_block, width = old_weight.shape
    strip = row_block * width // devices
    grid = Grid(groups, shards)
    me = lax.axis_index(AXES)
    by_tile = row_block == devices * SUB and width % 128 == 0 and devices % 2 == 0

    table = lax.dynamic_index_in_dim(jnp.asarray(order_table(grid)), me, 0, keepdims=False)
    chosen = (table % shards)[:, None] == jnp.arange(shards, dtype=jnp.int32)
    order = jnp.sum(jnp.where(chosen, new_owner, 0), axis=1) * groups + table // shards
    own = (grid.near - 1) * grid.side
    per_core = grid.near * grid.side

    if by_tile:
        half = row_block // 2
        held = [
            lax.all_gather(old_weight[start : start + half], AXES, axis=0, tiled=False)
            for start in (0, half)
        ]
        packed = pack_moments(old_first, old_second, new_owner, groups)
    else:
        held = lax.all_gather(old_weight, AXES, axis=0, tiled=False)
        slot_ids = jnp.arange(devices, dtype=jnp.int32)
        placing = jnp.take(new_owner, slot_ids % shards) * groups + slot_ids // shards
        both = jnp.stack([old_first, old_second]).astype(jnp.bfloat16)
        packed = jnp.take(
            jnp.transpose(both.reshape(2, devices, strip), (1, 0, 2)), placing, axis=0
        )
    arrived = lax.all_to_all(packed, AXES, split_axis=0, concat_axis=0, tiled=True)

    turned = cotangent.T

    def blocks_of(core, far, addend, cut):
        first = (far * grid.cores + core) * per_core
        return grad_blocks(
            tokens, turned, order, first, grid.near, grid.side, row_block, addend, cut
        )

    parts = reduce_rows(grid, blocks_of)
    if by_tile:
        projected, weight_rows = project(tokens, held, old_owner, order[own : own + 1])
        return (projected, *adam_rows(parts, arrived, weight_rows, old_owner))
    inverse = jnp.zeros((devices,), jnp.int32).at[old_owner].set(slot_ids)
    logical = jnp.transpose(
        jnp.take(held.reshape(devices, devices, strip), inverse, axis=0), (1, 0, 2)
    ).reshape(features, width)
    projected = jnp.dot(tokens, logical, preferred_element_type=jnp.float32).astype(jnp.bfloat16)
    weight_rows = lax.dynamic_slice_in_dim(logical, order[own] * row_block, row_block, 0)
    moved = jnp.transpose(jnp.take(arrived, inverse, axis=0), (1, 0, 2))
    first_rows, second_rows = moved.astype(jnp.float32).reshape(2, row_block, width)
    gradient = sum(part[0].astype(jnp.float32) for part in parts).T
    return (projected, *adam(weight_rows, first_rows, second_rows, gradient))


def solution(mesh):
    placed = P(AXES, None)
    return jax.shard_map(
        body,
        mesh=mesh,
        in_specs=(placed,) * 5 + (P(), P()),
        out_specs=(placed,) * 4,
        check_vma=False,
    )
```

```python
import functools
import jax
import jax.numpy as jnp
import numpy as np
from jax import lax
from jax.experimental import pallas as pl
from jax.experimental.pallas import tpu as pltpu
from jax.sharding import PartitionSpec as P

beta_one = 0.9
beta_two = 0.95
learn_rate = 0.001
decay_rate = 0.1
epsilon = 1e-08
correction_one = 1.0 - 0.9**10
correction_two = 1.0 - 0.95**10

AXES = ("rep", "fsdp")
GRANT = 48 * 1024 * 1024
SUB = 8


def cost(flops, moved):
    return pl.CostEstimate(flops=flops, bytes_accessed=moved, transcendentals=0)


def block_at(new_ref, groups, position):
    shards = new_ref.shape[0]
    return new_ref[lax.rem(position, shards)] * groups + lax.div(position, shards)


def grad_kernel(per_step, adds, row_ref, new_ref, *refs):
    token_refs, turned_ref, refs = refs[:per_step], refs[per_step], refs[per_step + 1 :]
    out_refs = refs[adds:]

    def write(out_ref):
        for slot, token_ref in enumerate(token_refs):
            block = jnp.dot(turned_ref[...], token_ref[...], preferred_element_type=jnp.float32)
            if adds:
                block = block + refs[0][slot].astype(jnp.float32)
            out_ref[slot] = block.astype(out_ref.dtype)

    if len(out_refs) == 1:
        write(out_refs[0])
        return
    for step, out_ref in enumerate(out_refs):
        pl.when(pl.program_id(0) == step)(functools.partial(write, out_ref))


def grad_blocks(tokens, turned, row, new_owner, first, steps, per_step, addend=None, cut=False):
    rows, features = tokens.shape
    width = turned.shape[0]
    blocks = steps * per_step
    groups = lax.axis_size("rep")
    row_block = features // (groups * new_owner.shape[0])
    if row_block % 128:
        chosen = row[first : first + blocks]
        chosen = jnp.take(new_owner, chosen % new_owner.shape[0]) * groups + (
            chosen // new_owner.shape[0]
        )
        whole = jnp.dot(turned, tokens, preferred_element_type=jnp.float32)
        parts = jnp.transpose(whole.reshape(width, features // row_block, row_block), (1, 0, 2))
        parts = jnp.take(parts, chosen, axis=0)
        if addend is not None:
            parts = parts + addend.astype(jnp.float32)
        parts = parts.astype(jnp.bfloat16)
        return list(jnp.split(parts, steps)) if cut else [parts]

    def token_map(slot):
        return lambda i, row_ref, new_ref: (
            0,
            block_at(new_ref, groups, row_ref[first + i * per_step + slot]),
        )

    block = pl.BlockSpec((per_step, width, row_block), lambda i, *_: (i, 0, 0))
    fixed = pl.BlockSpec((per_step, width, row_block), lambda i, *_: (0, 0, 0))
    added = [] if addend is None else [addend]
    outs = steps if cut else 1
    return pl.pallas_call(
        functools.partial(grad_kernel, per_step, len(added)),
        grid_spec=pltpu.PrefetchScalarGridSpec(
            num_scalar_prefetch=2,
            grid=(steps,),
            in_specs=[pl.BlockSpec((rows, row_block), token_map(s)) for s in range(per_step)]
            + [pl.BlockSpec((width, rows), lambda i, *_: (0, 0))]
            + [block] * len(added),
            out_specs=[fixed if cut else block] * outs,
        ),
        out_shape=[jax.ShapeDtypeStruct((blocks // outs, width, row_block), jnp.bfloat16)] * outs,
        compiler_params=pltpu.CompilerParams(vmem_limit_bytes=GRANT),
        cost_estimate=cost(
            2 * rows * width * blocks * row_block,
            2 * blocks * row_block * (rows + width * (1 + len(added))) + 2 * rows * width,
        ),
        name="weight_gradient",
    )(row, new_owner, *([tokens] * per_step), turned, *added)


def pack_kernel(groups, new_ref, first_ref, second_ref, out_ref):
    for slot in range(out_ref.shape[0]):
        block = block_at(new_ref, groups, slot)
        rows = pl.ds(pl.multiple_of(block * SUB, SUB), SUB)
        pair = jnp.concatenate([first_ref[rows, :], second_ref[rows, :]], axis=0)
        out_ref[slot] = pair.astype(out_ref.dtype)


def pack_moments(first, second, new_owner, groups):
    devices = new_owner.shape[0] * groups
    width = first.shape[1]
    return pl.pallas_call(
        functools.partial(pack_kernel, groups),
        in_specs=[
            pl.BlockSpec(memory_space=pltpu.SMEM),
            pl.BlockSpec(memory_space=pltpu.VMEM),
            pl.BlockSpec(memory_space=pltpu.VMEM),
        ],
        out_specs=pl.BlockSpec(memory_space=pltpu.VMEM),
        out_shape=jax.ShapeDtypeStruct((devices, 2 * SUB, width), jnp.bfloat16),
        cost_estimate=cost(0, 12 * first.size),
        name="pack_moments",
    )(new_owner, first, second)


def project_kernel(groups, first, own, row_ref, old_ref, new_ref, token_ref, *refs):
    piece_refs, (out_ref, rows_ref, held, logical, sems) = refs[:-5], refs[-5:]
    devices, row_block, _ = held.shape

    @pl.when(pl.program_id(0) == 0)
    def _():
        copies = []
        for piece_ref in piece_refs:
            for index in range(piece_ref.shape[0]):
                slot = len(copies)
                target = held.at[old_ref[row_ref[first + slot]]]
                copies.append(pltpu.make_async_copy(piece_ref.at[index], target, sems.at[slot]))
        for copy in copies:
            copy.start()
        for copy in copies:
            copy.wait()

        def place(pair, carry):
            for block in range(0, devices, 2):
                span = pl.ds(block * SUB, 2 * SUB)
                top = held[2 * pair, span, :]
                low = held[2 * pair + 1, span, :]
                for half in range(2):
                    part = slice(half * SUB, (half + 1) * SUB)
                    start = (block + half) * row_block + pair * 2 * SUB
                    logical[pl.ds(pl.multiple_of(start, 2 * SUB), 2 * SUB), :] = jnp.concatenate(
                        [top[part], low[part]], axis=0
                    )
            return carry

        lax.fori_loop(0, devices // 2, place, 0)
        start = block_at(new_ref, groups, row_ref[own]) * row_block
        start = pl.multiple_of(start, row_block)
        rows_ref[...] = logical[pl.ds(start, row_block), :]

    out_ref[...] = jnp.dot(
        token_ref[...], logical[...], preferred_element_type=jnp.float32
    ).astype(out_ref.dtype)


def project(tokens, pieces, row, first, own, old_owner, new_owner):
    rows, features = tokens.shape
    _, row_block, width = pieces[0].shape
    devices = old_owner.shape[0]
    tile = rows // 4
    return pl.pallas_call(
        functools.partial(project_kernel, devices // new_owner.shape[0], first, own),
        grid_spec=pltpu.PrefetchScalarGridSpec(
            num_scalar_prefetch=3,
            grid=(rows // tile,),
            in_specs=[pl.BlockSpec((tile, features), lambda i, *_: (i, 0))]
            + [pl.BlockSpec(memory_space=pl.ANY)] * len(pieces),
            out_specs=[
                pl.BlockSpec((tile, width), lambda i, *_: (i, 0)),
                pl.BlockSpec((row_block, width), lambda i, *_: (0, 0)),
            ],
            scratch_shapes=[
                pltpu.VMEM((devices, row_block, width), jnp.bfloat16),
                pltpu.VMEM((features, width), jnp.bfloat16),
                pltpu.SemaphoreType.DMA((devices,)),
            ],
        ),
        out_shape=[
            jax.ShapeDtypeStruct((rows, width), jnp.bfloat16),
            jax.ShapeDtypeStruct((row_block, width), jnp.bfloat16),
        ],
        compiler_params=pltpu.CompilerParams(vmem_limit_bytes=GRANT),
        cost_estimate=cost(
            2 * rows * width * features, 2 * (rows * features + features * width + rows * width)
        ),
        name="project",
    )(row, old_owner, new_owner, tokens, *pieces)


def adam(weight_rows, first_rows, second_rows, gradient):
    first_next = beta_one * first_rows + (1.0 - beta_one) * gradient
    second_next = beta_two * second_rows + (1.0 - beta_two) * gradient * gradient
    step_size = first_next / correction_one / (jnp.sqrt(second_next / correction_two) + epsilon)
    updated = (
        weight_rows.astype(jnp.float32) * (1.0 - learn_rate * decay_rate) - learn_rate * step_size
    ).astype(jnp.bfloat16)
    return updated, first_next, second_next


def adam_kernel(owner_ref, moments_ref, weight_ref, *refs):
    part_refs, (new_ref, first_ref, second_ref, gradient, inverse_ref) = refs[:-5], refs[-5:]
    for slot in range(moments_ref.shape[0]):
        inverse_ref[owner_ref[slot]] = slot
    total = part_refs[0][0].astype(jnp.float32)
    for part_ref in part_refs[1:]:
        total = total + part_ref[0].astype(jnp.float32)
    gradient[...] = total.T
    for pair in range(moments_ref.shape[0] // 2):
        even = moments_ref[inverse_ref[2 * pair]].astype(jnp.float32)
        odd = moments_ref[inverse_ref[2 * pair + 1]].astype(jnp.float32)
        rows = pl.ds(pair * 2 * SUB, 2 * SUB)
        new_ref[rows, :], first_ref[rows, :], second_ref[rows, :] = adam(
            weight_ref[rows, :],
            jnp.concatenate([even[:SUB], odd[:SUB]], axis=0),
            jnp.concatenate([even[SUB:], odd[SUB:]], axis=0),
            gradient[rows, :],
        )


def adam_rows(parts, moments, weight_rows, owners):
    row_block, width = weight_rows.shape
    whole = pl.BlockSpec((row_block, width), lambda i, *_: (0, 0))
    return pl.pallas_call(
        adam_kernel,
        grid_spec=pltpu.PrefetchScalarGridSpec(
            num_scalar_prefetch=1,
            grid=(1,),
            in_specs=[pl.BlockSpec(moments.shape, lambda i, *_: (0, 0, 0)), whole]
            + [pl.BlockSpec((1, width, row_block), lambda i, *_: (0, 0, 0))] * len(parts),
            out_specs=[whole] * 3,
            scratch_shapes=[
                pltpu.VMEM((row_block, width), jnp.float32),
                pltpu.SMEM((moments.shape[0],), jnp.int32),
            ],
        ),
        out_shape=[
            jax.ShapeDtypeStruct((row_block, width), jnp.bfloat16),
            jax.ShapeDtypeStruct((row_block, width), jnp.float32),
            jax.ShapeDtypeStruct((row_block, width), jnp.float32),
        ],
        compiler_params=pltpu.CompilerParams(vmem_limit_bytes=GRANT),
        cost_estimate=cost(20 * row_block * width, 16 * row_block * width),
        name="adam_rows",
    )(owners, moments, weight_rows, *parts)


class Grid:
    def __init__(self, groups, shards):
        self.shards = shards
        self.cores = 2 if groups % 2 == 0 else 1
        self.minor = 2 if shards % 2 == 0 else 1
        self.outer = groups // self.cores
        self.far = shards // self.minor
        self.swaps = self.cores == 2 and self.minor == self.outer
        self.near, self.side = self.minor, self.outer

    def moved(self, position, core=0, near=0, side=0, far=0):
        group, shard = position // self.shards, position % self.shards
        outer, on = group // self.cores, (group % self.cores + core) % self.cores
        depth, minor = shard // self.minor, shard % self.minor
        swapped = on if self.swaps else 0
        minor = (minor + near + (side - near) * swapped) % self.minor
        outer = (outer + side + (near - side) * swapped) % self.outer
        depth = (depth + far) % self.far
        return (outer * self.cores + on) * self.shards + depth * self.minor + minor

    def send(self, value, **steps):
        devices = self.outer * self.cores * self.shards
        pairs = [(p, self.moved(p, **steps)) for p in range(devices)]
        return lax.ppermute(value, AXES, pairs)


def rounded_sum(*terms):
    total = terms[0].astype(jnp.float32)
    for term in terms[1:]:
        total = total + term.astype(jnp.float32)
    return total.astype(terms[0].dtype)


def chunks(grid):
    half = grid.far // 2
    return [sorted({d, (grid.far - d) % grid.far}) for d in range(half + 1)]


def tables(grid, devices):
    sums = [
        dict(core=core, near=near, side=side, far=far)
        for chunk in chunks(grid)
        for core in range(grid.cores)
        for near in [*range(1, grid.near), 0]
        for side in range(grid.side)
        for far in chunk
    ]
    shards = [
        dict(core=-core, near=-near, side=-side, far=-far)
        for chunk in chunks(grid)
        for core in range(grid.cores)
        for near in range(grid.near)
        for side in range(grid.side)
        for far in chunk
    ]
    return np.array(
        [[grid.moved(p, **step) for step in sums + shards] for p in range(devices)], np.int32
    )


def reduce_rows(grid, blocks_of):
    last = []
    start = grid.far
    for chunk in reversed(chunks(grid)):
        count = len(chunk)
        start -= count
        addend = None
        if grid.cores > 1:
            addend = grid.send(blocks_of(1, start, count, None, False)[0], core=1)
        parts = blocks_of(0, start, count, addend, True)
        kept = [parts[-1]]
        for step, part in enumerate(parts[:-1], 1):
            kept.append(grid.send(part, near=step))
        ends = list(kept)
        for step in range(1, grid.side):
            cut = slice(step * count, (step + 1) * count)
            ends.append(grid.send(rounded_sum(*[t[cut] for t in kept]), side=step))
        if chunk == [0]:
            last.extend(ends)
            continue
        for index, far in enumerate(chunk):
            cut = slice(index, index + 1)
            last.append(grid.send(rounded_sum(*[t[cut] for t in ends]), far=far))
    return last


def gather_shards(grid, own):
    arrived = {far: grid.send(own, far=far) for far in range(1, grid.far)}
    arrived[0] = own
    pieces = []
    for chunk in chunks(grid):
        base = joined([arrived[far] for far in chunk])
        plane = joined([base] + [grid.send(base, side=step) for step in range(1, grid.side)])
        both = [plane] + [grid.send(plane, near=step) for step in range(1, grid.near)]
        pieces += both
        for core in range(1, grid.cores):
            pieces += [grid.send(part, core=core) for part in both]
    return pieces


def joined(arrays):
    return arrays[0] if len(arrays) == 1 else jnp.concatenate(arrays, axis=0)


def body(tokens, cotangent, old_weight, old_first, old_second, old_owner, new_owner):
    devices = lax.axis_size(AXES)
    groups = lax.axis_size("rep")
    shards = lax.axis_size("fsdp")
    features = tokens.shape[1]
    row_block, width = old_weight.shape
    strip = row_block * width // devices
    grid = Grid(groups, shards)
    me = lax.axis_index(AXES)
    by_tile = row_block == devices * SUB and width % 128 == 0 and devices % 2 == 0

    row = lax.dynamic_index_in_dim(jnp.asarray(tables(grid, devices)), me, 0, keepdims=False)
    per_far = grid.near * grid.side
    own = (grid.near - 1) * grid.side

    pieces = gather_shards(grid, old_weight[None])
    if by_tile:
        packed = pack_moments(old_first, old_second, new_owner, groups)
    else:
        slot_ids = jnp.arange(devices, dtype=jnp.int32)
        placing = jnp.take(new_owner, slot_ids % shards) * groups + slot_ids // shards
        both = jnp.stack([old_first, old_second]).astype(jnp.bfloat16)
        packed = jnp.take(
            jnp.transpose(both.reshape(2, devices, strip), (1, 0, 2)), placing, axis=0
        )
    arrived = lax.all_to_all(packed, AXES, split_axis=0, concat_axis=0, tiled=True)

    turned = cotangent.T

    def blocks_of(core, start, count, addend, cut):
        first = (start * grid.cores + core * count) * per_far
        per_step = grid.side * count
        return grad_blocks(
            tokens, turned, row, new_owner, first, grid.near, per_step, addend, cut
        )

    parts = reduce_rows(grid, blocks_of)
    if by_tile:
        projected, weight_rows = project(tokens, pieces, row, devices, own, old_owner, new_owner)
        return (projected, *adam_rows(parts, arrived, weight_rows, old_owner))
    inverse = jnp.zeros((devices,), jnp.int32).at[old_owner].set(slot_ids)
    held = jnp.zeros((devices, devices, strip), jnp.bfloat16)
    held = held.at[jnp.take(old_owner, row[devices:])].set(
        joined(pieces).reshape(devices, devices, strip)
    )
    logical = jnp.transpose(held, (1, 0, 2)).reshape(features, width)
    projected = jnp.dot(tokens, logical, preferred_element_type=jnp.float32).astype(jnp.bfloat16)
    own_block = jnp.take(placing, me)
    weight_rows = lax.dynamic_slice_in_dim(logical, own_block * row_block, row_block, 0)
    moved = jnp.transpose(jnp.take(arrived, inverse, axis=0), (1, 0, 2))
    first_rows, second_rows = moved.astype(jnp.float32).reshape(2, row_block, width)
    gradient = sum(part[0].astype(jnp.float32) for part in parts).T
    return (projected, *adam(weight_rows, first_rows, second_rows, gradient))


def solution(mesh):
    placed = P(AXES, None)
    return jax.shard_map(
        body,
        mesh=mesh,
        in_specs=(placed,) * 5 + (P(), P()),
        out_specs=(placed,) * 4,
        check_vma=False,
    )
```

```python
import functools
import jax
import jax.numpy as jnp
import numpy as np
from jax import lax
from jax.experimental import pallas as pl
from jax.experimental.pallas import tpu as pltpu
from jax.sharding import PartitionSpec as P

beta_one = 0.9
beta_two = 0.95
learn_rate = 0.001
decay_rate = 0.1
epsilon = 1e-08
correction_one = 1.0 - 0.9**10
correction_two = 1.0 - 0.95**10

AXES = ("rep", "fsdp")
MIB = 1024 * 1024
SUB = 8


def cost(flops, moved):
    return pl.CostEstimate(flops=flops, bytes_accessed=moved, transcendentals=0)


def block_at(new_ref, groups, position):
    shards = new_ref.shape[0]
    return new_ref[lax.rem(position, shards)] * groups + lax.div(position, shards)


def grad_kernel(per_step, adds, outs, row_ref, new_ref, *refs):
    token_refs, turned_ref, refs = refs[:per_step], refs[per_step], refs[per_step + 1 :]
    out_refs = refs[-outs:]
    step = pl.program_id(0)

    def write(out_ref, start):
        for slot, token_ref in enumerate(token_refs):
            block = jnp.dot(turned_ref[...], token_ref[...], preferred_element_type=jnp.float32)
            if adds:
                block = block + refs[0][step * per_step + slot].astype(jnp.float32)
            out_ref[start + slot] = block.astype(out_ref.dtype)

    if outs == 1:
        write(out_refs[0], step * per_step)
        return
    for part, out_ref in enumerate(out_refs):
        pl.when(step == part)(functools.partial(write, out_ref, 0))


def grad_blocks(
    tokens, turned, row, new_owner, first, steps, per_step, addend=None, cut=False, after=()
):
    rows, features = tokens.shape
    width = turned.shape[0]
    blocks = steps * per_step
    groups = lax.axis_size("rep")
    row_block = features // (groups * new_owner.shape[0])
    if row_block % 128:
        chosen = row[first : first + blocks]
        chosen = jnp.take(new_owner, chosen % new_owner.shape[0]) * groups + (
            chosen // new_owner.shape[0]
        )
        whole = jnp.dot(turned, tokens, preferred_element_type=jnp.float32)
        parts = jnp.transpose(whole.reshape(width, features // row_block, row_block), (1, 0, 2))
        parts = jnp.take(parts, chosen, axis=0)
        if addend is not None:
            parts = parts + addend.astype(jnp.float32)
        parts = parts.astype(jnp.bfloat16)
        return list(jnp.split(parts, steps)) if cut else [parts]

    def token_map(slot):
        return lambda i, row_ref, new_ref: (
            0,
            block_at(new_ref, groups, row_ref[first + i * per_step + slot]),
        )

    whole = pl.BlockSpec(memory_space=pltpu.VMEM)
    added = [] if addend is None else [addend]
    outs = steps if cut else 1
    return pl.pallas_call(
        functools.partial(grad_kernel, per_step, len(added), outs),
        grid_spec=pltpu.PrefetchScalarGridSpec(
            num_scalar_prefetch=2,
            grid=(steps,),
            in_specs=[pl.BlockSpec((rows, row_block), token_map(s)) for s in range(per_step)]
            + [whole] * (1 + len(added))
            + [pl.BlockSpec(memory_space=pl.ANY)] * len(after),
            out_specs=[whole] * outs,
        ),
        out_shape=[jax.ShapeDtypeStruct((blocks // outs, width, row_block), jnp.bfloat16)] * outs,
        compiler_params=pltpu.CompilerParams(vmem_limit_bytes=46 * MIB),
        cost_estimate=cost(
            2 * rows * width * blocks * row_block,
            2 * blocks * row_block * (rows + width * (1 + len(added))) + 2 * rows * width,
        ),
        name="weight_gradient",
    )(row, new_owner, *([tokens] * per_step), turned, *added, *after)


def pack_kernel(groups, new_ref, first_ref, second_ref, out_ref):
    for slot in range(out_ref.shape[0]):
        block = block_at(new_ref, groups, slot)
        rows = pl.ds(pl.multiple_of(block * SUB, SUB), SUB)
        pair = jnp.concatenate([first_ref[rows, :], second_ref[rows, :]], axis=0)
        out_ref[slot] = pair.astype(out_ref.dtype)


def pack_moments(first, second, new_owner, groups):
    devices = new_owner.shape[0] * groups
    width = first.shape[1]
    return pl.pallas_call(
        functools.partial(pack_kernel, groups),
        in_specs=[
            pl.BlockSpec(memory_space=pltpu.SMEM),
            pl.BlockSpec(memory_space=pltpu.VMEM),
            pl.BlockSpec(memory_space=pltpu.VMEM),
        ],
        out_specs=pl.BlockSpec(memory_space=pltpu.VMEM),
        out_shape=jax.ShapeDtypeStruct((devices, 2 * SUB, width), jnp.bfloat16),
        cost_estimate=cost(0, 12 * first.size),
        name="pack_moments",
    )(new_owner, first, second)


def project_kernel(groups, first, own, row_ref, old_ref, new_ref, token_ref, *refs):
    piece_refs, (out_ref, rows_ref, held, logical, sems) = refs[:-5], refs[-5:]
    devices, row_block, _ = held.shape

    @pl.when(pl.program_id(0) == 0)
    def _():
        copies = []
        for piece_ref in piece_refs:
            for index in range(piece_ref.shape[0]):
                slot = len(copies)
                target = held.at[old_ref[row_ref[first + slot]]]
                copies.append(pltpu.make_async_copy(piece_ref.at[index], target, sems.at[slot]))
        for copy in copies:
            copy.start()
        for copy in copies:
            copy.wait()

        def place(pair, carry):
            for block in range(0, devices, 2):
                span = pl.ds(block * SUB, 2 * SUB)
                top = held[2 * pair, span, :]
                low = held[2 * pair + 1, span, :]
                for half in range(2):
                    part = slice(half * SUB, (half + 1) * SUB)
                    start = (block + half) * row_block + pair * 2 * SUB
                    logical[pl.ds(pl.multiple_of(start, 2 * SUB), 2 * SUB), :] = jnp.concatenate(
                        [top[part], low[part]], axis=0
                    )
            return carry

        lax.fori_loop(0, devices // 2, place, 0)
        start = block_at(new_ref, groups, row_ref[own]) * row_block
        start = pl.multiple_of(start, row_block)
        rows_ref[...] = logical[pl.ds(start, row_block), :]

    out_ref[...] = jnp.dot(
        token_ref[...], logical[...], preferred_element_type=jnp.float32
    ).astype(out_ref.dtype)


def project(tokens, pieces, row, first, own, old_owner, new_owner):
    rows, features = tokens.shape
    _, row_block, width = pieces[0].shape
    devices = old_owner.shape[0]
    tile = rows // 4
    return pl.pallas_call(
        functools.partial(project_kernel, devices // new_owner.shape[0], first, own),
        grid_spec=pltpu.PrefetchScalarGridSpec(
            num_scalar_prefetch=3,
            grid=(rows // tile,),
            in_specs=[pl.BlockSpec((tile, features), lambda i, *_: (i, 0))]
            + [pl.BlockSpec(memory_space=pl.ANY)] * len(pieces),
            out_specs=[
                pl.BlockSpec((tile, width), lambda i, *_: (i, 0)),
                pl.BlockSpec((row_block, width), lambda i, *_: (0, 0)),
            ],
            scratch_shapes=[
                pltpu.VMEM((devices, row_block, width), jnp.bfloat16),
                pltpu.VMEM((features, width), jnp.bfloat16),
                pltpu.SemaphoreType.DMA((devices,)),
            ],
        ),
        out_shape=[
            jax.ShapeDtypeStruct((rows, width), jnp.bfloat16),
            jax.ShapeDtypeStruct((row_block, width), jnp.bfloat16),
        ],
        compiler_params=pltpu.CompilerParams(vmem_limit_bytes=46 * MIB),
        cost_estimate=cost(
            2 * rows * width * features, 2 * (rows * features + features * width + rows * width)
        ),
        name="project",
    )(row, old_owner, new_owner, tokens, *pieces)


def adam(weight_rows, first_rows, second_rows, gradient):
    first_next = beta_one * first_rows + (1.0 - beta_one) * gradient
    second_next = beta_two * second_rows + (1.0 - beta_two) * gradient * gradient
    step_size = first_next / correction_one / (jnp.sqrt(second_next / correction_two) + epsilon)
    updated = (
        weight_rows.astype(jnp.float32) * (1.0 - learn_rate * decay_rate) - learn_rate * step_size
    ).astype(jnp.bfloat16)
    return updated, first_next, second_next


def adam_kernel(owner_ref, moments_ref, weight_ref, *refs):
    part_refs, (new_ref, first_ref, second_ref, gradient, inverse_ref) = refs[:-5], refs[-5:]
    for slot in range(moments_ref.shape[0]):
        inverse_ref[owner_ref[slot]] = slot
    total = part_refs[0][0].astype(jnp.float32)
    for part_ref in part_refs[1:]:
        total = total + part_ref[0].astype(jnp.float32)
    gradient[...] = total.T
    for pair in range(moments_ref.shape[0] // 2):
        even = moments_ref[inverse_ref[2 * pair]].astype(jnp.float32)
        odd = moments_ref[inverse_ref[2 * pair + 1]].astype(jnp.float32)
        rows = pl.ds(pair * 2 * SUB, 2 * SUB)
        new_ref[rows, :], first_ref[rows, :], second_ref[rows, :] = adam(
            weight_ref[rows, :],
            jnp.concatenate([even[:SUB], odd[:SUB]], axis=0),
            jnp.concatenate([even[SUB:], odd[SUB:]], axis=0),
            gradient[rows, :],
        )


def adam_rows(parts, moments, weight_rows, owners):
    row_block, width = weight_rows.shape
    whole = pl.BlockSpec(memory_space=pltpu.VMEM)
    return pl.pallas_call(
        adam_kernel,
        in_specs=[pl.BlockSpec(memory_space=pltpu.SMEM)] + [whole] * (2 + len(parts)),
        out_specs=[whole] * 3,
        scratch_shapes=[
            pltpu.VMEM((row_block, width), jnp.float32),
            pltpu.SMEM((moments.shape[0],), jnp.int32),
        ],
        out_shape=[
            jax.ShapeDtypeStruct((row_block, width), jnp.bfloat16),
            jax.ShapeDtypeStruct((row_block, width), jnp.float32),
            jax.ShapeDtypeStruct((row_block, width), jnp.float32),
        ],
        compiler_params=pltpu.CompilerParams(vmem_limit_bytes=12 * MIB),
        cost_estimate=cost(20 * row_block * width, 16 * row_block * width),
        name="adam_rows",
    )(owners, moments, weight_rows, *parts)


class Grid:
    def __init__(self, groups, shards):
        self.shards = shards
        self.cores = 2 if groups % 2 == 0 else 1
        self.minor = 2 if shards % 2 == 0 else 1
        self.outer = groups // self.cores
        self.far = shards // self.minor
        self.swaps = self.cores == 2 and self.minor == self.outer
        self.near, self.side = self.minor, self.outer

    def moved(self, position, core=0, near=0, side=0, far=0):
        group, shard = position // self.shards, position % self.shards
        outer, on = group // self.cores, (group % self.cores + core) % self.cores
        depth, minor = shard // self.minor, shard % self.minor
        swapped = on if self.swaps else 0
        minor = (minor + near + (side - near) * swapped) % self.minor
        outer = (outer + side + (near - side) * swapped) % self.outer
        depth = (depth + far) % self.far
        return (outer * self.cores + on) * self.shards + depth * self.minor + minor

    def send(self, value, **steps):
        devices = self.outer * self.cores * self.shards
        pairs = [(p, self.moved(p, **steps)) for p in range(devices)]
        return lax.ppermute(value, AXES, pairs)


def sum_kernel(start, count, terms, *refs):
    out_ref = refs[-1]
    total = refs[0][start : start + count].astype(jnp.float32)
    for ref in refs[1:terms]:
        total = total + ref[start : start + count].astype(jnp.float32)
    out_ref[...] = total.astype(out_ref.dtype)


def rounded_sum(terms, start, count, after=()):
    shape = (count, *terms[0].shape[1:])
    if shape[-1] % 128:
        total = sum(term[start : start + count].astype(jnp.float32) for term in terms)
        return total.astype(terms[0].dtype)
    whole = pl.BlockSpec(memory_space=pltpu.VMEM)
    size = count * shape[1] * shape[2]
    return pl.pallas_call(
        functools.partial(sum_kernel, start, count, len(terms)),
        in_specs=[whole] * len(terms) + [pl.BlockSpec(memory_space=pl.ANY)] * len(after),
        out_specs=whole,
        out_shape=jax.ShapeDtypeStruct(shape, terms[0].dtype),
        compiler_params=pltpu.CompilerParams(vmem_limit_bytes=12 * MIB),
        cost_estimate=cost(size * len(terms), 2 * size * (len(terms) + 1)),
        name="add_blocks",
    )(*terms, *after)


def chunks(grid):
    half = grid.far // 2
    return [sorted({d, (grid.far - d) % grid.far}) for d in range(half + 1)]


def tables(grid, devices):
    sums = [
        dict(core=core, near=near, side=side, far=far)
        for chunk in chunks(grid)
        for core in range(grid.cores)
        for near in [*range(1, grid.near), 0]
        for side in range(grid.side)
        for far in chunk
    ]
    shards = [
        dict(core=-core, near=-near, side=-side, far=-far)
        for chunk in chunks(grid)
        for core in range(grid.cores)
        for near in range(grid.near)
        for side in range(grid.side)
        for far in chunk
    ]
    return np.array(
        [[grid.moved(p, **step) for step in sums + shards] for p in range(devices)], np.int32
    )


def reduce_rows(grid, blocks_of, project_now):
    plan = []
    start = 0
    for number, chunk in enumerate(chunks(grid)):
        plan.insert(0, (number, chunk, start))
        start += len(chunk)
    addends = {}
    if grid.cores > 1:
        for number, chunk, start in plan:
            block = blocks_of(1, number, start, len(chunk), None, False)[0]
            addends[number] = grid.send(block, core=1)
    held = {}
    for number, chunk, start in plan:
        parts = blocks_of(0, number, start, len(chunk), addends.get(number), True)
        held[number] = [parts[-1]]
        for step, part in enumerate(parts[:-1], 1):
            held[number].append(grid.send(part, near=step))
    projection = project_now()
    last = []
    for number, chunk, _ in plan:
        count = len(chunk)
        kept = held[number]
        ends = list(kept)
        for step in range(1, grid.side):
            part = rounded_sum(kept, step * count, count, projection[1:])
            ends.append(grid.send(part, side=step))
        held[number] = ends
    for number, chunk, _ in plan:
        ends = held[number]
        if chunk == [0]:
            last.extend(ends)
            continue
        for index, far in enumerate(chunk):
            last.append(grid.send(rounded_sum(ends, index, 1), far=far))
    return last, projection


def gather_shards(grid, own):
    arrived = {far: grid.send(own, far=far) for far in range(1, grid.far)}
    arrived[0] = own
    pieces, marks = [], []
    for chunk in chunks(grid):
        base = joined([arrived[far] for far in chunk])
        sides = [grid.send(base, side=step) for step in range(1, grid.side)]
        plane = joined([base] + sides)
        nears = [grid.send(plane, near=step) for step in range(1, grid.near)]
        both = [plane] + nears
        marks.append((sides, nears, [arrived[far] for far in chunk]))
        pieces += both
        for core in range(1, grid.cores):
            pieces += [grid.send(part, core=core) for part in both]
    return pieces, marks


def joined(arrays):
    return arrays[0] if len(arrays) == 1 else jnp.concatenate(arrays, axis=0)


def body(tokens, cotangent, old_weight, old_first, old_second, old_owner, new_owner):
    devices = lax.axis_size(AXES)
    groups = lax.axis_size("rep")
    shards = lax.axis_size("fsdp")
    features = tokens.shape[1]
    row_block, width = old_weight.shape
    strip = row_block * width // devices
    grid = Grid(groups, shards)
    me = lax.axis_index(AXES)
    by_tile = row_block == devices * SUB and width % 128 == 0 and devices % 2 == 0

    row = lax.dynamic_index_in_dim(jnp.asarray(tables(grid, devices)), me, 0, keepdims=False)
    per_far = grid.near * grid.side
    own = (grid.near - 1) * grid.side

    pieces, marks = gather_shards(grid, old_weight[None])
    if by_tile:
        packed = pack_moments(old_first, old_second, new_owner, groups)
    else:
        slot_ids = jnp.arange(devices, dtype=jnp.int32)
        placing = jnp.take(new_owner, slot_ids % shards) * groups + slot_ids // shards
        both = jnp.stack([old_first, old_second]).astype(jnp.bfloat16)
        packed = jnp.take(
            jnp.transpose(both.reshape(2, devices, strip), (1, 0, 2)), placing, axis=0
        )
    arrived = lax.all_to_all(packed, AXES, split_axis=0, concat_axis=0, tiled=True)

    turned = cotangent.T

    waits = {
        (1, 2): [packed, *marks[0][0]],
        (1, 1): marks[1][2],
        (1, 0): [*marks[1][0], *marks[2][2]],
        (0, 2): [*marks[0][1], *marks[2][0]],
        (0, 0): [*marks[1][1], arrived],
    }
    if not by_tile:
        waits = {}
    done = []

    def blocks_of(core, chunk, start, count, addend, cut):
        first = (start * grid.cores + core * count) * per_far
        per_step = grid.side * count
        after = [*waits.get((core, chunk), ()), *done[-1:]]
        blocks = grad_blocks(
            tokens, turned, row, new_owner, first, grid.near, per_step, addend, cut, after
        )
        done.append(blocks[0])
        return blocks

    def project_now():
        if by_tile:
            return project(tokens, pieces, row, devices, own, old_owner, new_owner)
        return ()

    parts, projection = reduce_rows(grid, blocks_of, project_now)
    if by_tile:
        projected, weight_rows = projection
        return (projected, *adam_rows(parts, arrived, weight_rows, old_owner))
    inverse = jnp.zeros((devices,), jnp.int32).at[old_owner].set(slot_ids)
    held = jnp.zeros((devices, devices, strip), jnp.bfloat16)
    held = held.at[jnp.take(old_owner, row[devices:])].set(
        joined(pieces).reshape(devices, devices, strip)
    )
    logical = jnp.transpose(held, (1, 0, 2)).reshape(features, width)
    projected = jnp.dot(tokens, logical, preferred_element_type=jnp.float32).astype(jnp.bfloat16)
    own_block = jnp.take(placing, me)
    weight_rows = lax.dynamic_slice_in_dim(logical, own_block * row_block, row_block, 0)
    moved = jnp.transpose(jnp.take(arrived, inverse, axis=0), (1, 0, 2))
    first_rows, second_rows = moved.astype(jnp.float32).reshape(2, row_block, width)
    gradient = sum(part[0].astype(jnp.float32) for part in parts).T
    return (projected, *adam(weight_rows, first_rows, second_rows, gradient))


def solution(mesh):
    placed = P(AXES, None)
    return jax.shard_map(
        body,
        mesh=mesh,
        in_specs=(placed,) * 5 + (P(), P()),
        out_specs=(placed,) * 4,
        check_vma=False,
    )
```

```python
import functools
import jax
import jax.numpy as jnp
import numpy as np
from jax import lax
from jax.experimental import pallas as pl
from jax.experimental.pallas import tpu as pltpu
from jax.sharding import PartitionSpec as P

beta_one = 0.9
beta_two = 0.95
learn_rate = 0.001
decay_rate = 0.1
epsilon = 1e-08
correction_one = 1.0 - 0.9**10
correction_two = 1.0 - 0.95**10

AXES = ("rep", "fsdp")
MIB = 1024 * 1024
SUB = 8


def cost(flops, moved):
    return pl.CostEstimate(flops=flops, bytes_accessed=moved, transcendentals=0)


def block_at(new_ref, groups, position):
    shards = new_ref.shape[0]
    return new_ref[lax.rem(position, shards)] * groups + lax.div(position, shards)


def grad_kernel(per_step, adds, outs, row_ref, new_ref, *refs):
    token_refs, turned_ref, refs = refs[:per_step], refs[per_step], refs[per_step + 1 :]
    out_refs = refs[-outs:]

    def write(out_ref):
        for slot, token_ref in enumerate(token_refs):
            block = jnp.dot(turned_ref[...], token_ref[...], preferred_element_type=jnp.float32)
            if adds:
                block = block + refs[0][slot].astype(jnp.float32)
            out_ref[slot] = block.astype(out_ref.dtype)

    if outs == 1:
        write(out_refs[0])
        return
    for part, out_ref in enumerate(out_refs):
        pl.when(pl.program_id(0) == part)(functools.partial(write, out_ref))


def grad_blocks(
    tokens, turned, row, new_owner, first, steps, per_step, addend=None, cut=False, after=()
):
    rows, features = tokens.shape
    width = turned.shape[0]
    blocks = steps * per_step
    groups = lax.axis_size("rep")
    row_block = features // (groups * new_owner.shape[0])
    if row_block % 128:
        chosen = row[first : first + blocks]
        chosen = jnp.take(new_owner, chosen % new_owner.shape[0]) * groups + (
            chosen // new_owner.shape[0]
        )
        whole = jnp.dot(turned, tokens, preferred_element_type=jnp.float32)
        parts = jnp.transpose(whole.reshape(width, features // row_block, row_block), (1, 0, 2))
        parts = jnp.take(parts, chosen, axis=0)
        if addend is not None:
            parts = parts + addend.astype(jnp.float32)
        parts = parts.astype(jnp.bfloat16)
        return list(jnp.split(parts, steps)) if cut else [parts]

    def token_map(slot):
        return lambda i, row_ref, new_ref: (
            0,
            block_at(new_ref, groups, row_ref[first + i * per_step + slot]),
        )

    block = pl.BlockSpec((per_step, width, row_block), lambda i, *_: (i, 0, 0))
    fixed = pl.BlockSpec((per_step, width, row_block), lambda i, *_: (0, 0, 0))
    added = [] if addend is None else [addend]
    outs = steps if cut else 1
    return pl.pallas_call(
        functools.partial(grad_kernel, per_step, len(added), outs),
        grid_spec=pltpu.PrefetchScalarGridSpec(
            num_scalar_prefetch=2,
            grid=(steps,),
            in_specs=[pl.BlockSpec((rows, row_block), token_map(s)) for s in range(per_step)]
            + [pl.BlockSpec((width, rows), lambda i, *_: (0, 0))]
            + [block] * len(added)
            + [pl.BlockSpec(memory_space=pl.ANY)] * len(after),
            out_specs=[fixed if cut else block] * outs,
        ),
        out_shape=[jax.ShapeDtypeStruct((blocks // outs, width, row_block), jnp.bfloat16)] * outs,
        compiler_params=pltpu.CompilerParams(vmem_limit_bytes=46 * MIB),
        cost_estimate=cost(
            2 * rows * width * blocks * row_block,
            2 * blocks * row_block * (rows + width * (1 + len(added))) + 2 * rows * width,
        ),
        name="weight_gradient",
    )(row, new_owner, *([tokens] * per_step), turned, *added, *after)


def pack_kernel(groups, new_ref, first_ref, second_ref, out_ref):
    for slot in range(out_ref.shape[0]):
        block = block_at(new_ref, groups, slot)
        rows = pl.ds(pl.multiple_of(block * SUB, SUB), SUB)
        pair = jnp.concatenate([first_ref[rows, :], second_ref[rows, :]], axis=0)
        out_ref[slot] = pair.astype(out_ref.dtype)


def pack_moments(first, second, new_owner, groups):
    devices = new_owner.shape[0] * groups
    width = first.shape[1]
    return pl.pallas_call(
        functools.partial(pack_kernel, groups),
        in_specs=[
            pl.BlockSpec(memory_space=pltpu.SMEM),
            pl.BlockSpec(memory_space=pltpu.VMEM),
            pl.BlockSpec(memory_space=pltpu.VMEM),
        ],
        out_specs=pl.BlockSpec(memory_space=pltpu.VMEM),
        out_shape=jax.ShapeDtypeStruct((devices, 2 * SUB, width), jnp.bfloat16),
        cost_estimate=cost(0, 12 * first.size),
        name="pack_moments",
    )(new_owner, first, second)


def project_kernel(groups, first, own, row_ref, old_ref, new_ref, token_ref, *refs):
    piece_refs, (out_ref, rows_ref, held, logical, sems) = refs[:-5], refs[-5:]
    devices, row_block, _ = held.shape

    @pl.when(pl.program_id(0) == 0)
    def _():
        copies = []
        for piece_ref in piece_refs:
            for index in range(piece_ref.shape[0]):
                slot = len(copies)
                target = held.at[old_ref[row_ref[first + slot]]]
                copies.append(pltpu.make_async_copy(piece_ref.at[index], target, sems.at[slot]))
        for copy in copies:
            copy.start()
        for copy in copies:
            copy.wait()

        def place(pair, carry):
            for block in range(0, devices, 2):
                span = pl.ds(block * SUB, 2 * SUB)
                top = held[2 * pair, span, :]
                low = held[2 * pair + 1, span, :]
                for half in range(2):
                    part = slice(half * SUB, (half + 1) * SUB)
                    start = (block + half) * row_block + pair * 2 * SUB
                    logical[pl.ds(pl.multiple_of(start, 2 * SUB), 2 * SUB), :] = jnp.concatenate(
                        [top[part], low[part]], axis=0
                    )
            return carry

        lax.fori_loop(0, devices // 2, place, 0)
        start = block_at(new_ref, groups, row_ref[own]) * row_block
        start = pl.multiple_of(start, row_block)
        rows_ref[...] = logical[pl.ds(start, row_block), :]

    out_ref[...] = jnp.dot(
        token_ref[...], logical[...], preferred_element_type=jnp.float32
    ).astype(out_ref.dtype)


def project(tokens, pieces, row, first, own, old_owner, new_owner):
    rows, features = tokens.shape
    _, row_block, width = pieces[0].shape
    devices = old_owner.shape[0]
    tile = rows // 4
    return pl.pallas_call(
        functools.partial(project_kernel, devices // new_owner.shape[0], first, own),
        grid_spec=pltpu.PrefetchScalarGridSpec(
            num_scalar_prefetch=3,
            grid=(rows // tile,),
            in_specs=[pl.BlockSpec((tile, features), lambda i, *_: (i, 0))]
            + [pl.BlockSpec(memory_space=pl.ANY)] * len(pieces),
            out_specs=[
                pl.BlockSpec((tile, width), lambda i, *_: (i, 0)),
                pl.BlockSpec((row_block, width), lambda i, *_: (0, 0)),
            ],
            scratch_shapes=[
                pltpu.VMEM((devices, row_block, width), jnp.bfloat16),
                pltpu.VMEM((features, width), jnp.bfloat16),
                pltpu.SemaphoreType.DMA((devices,)),
            ],
        ),
        out_shape=[
            jax.ShapeDtypeStruct((rows, width), jnp.bfloat16),
            jax.ShapeDtypeStruct((row_block, width), jnp.bfloat16),
        ],
        compiler_params=pltpu.CompilerParams(vmem_limit_bytes=46 * MIB),
        cost_estimate=cost(
            2 * rows * width * features, 2 * (rows * features + features * width + rows * width)
        ),
        name="project",
    )(row, old_owner, new_owner, tokens, *pieces)


def adam(weight_rows, first_rows, second_rows, gradient):
    first_next = beta_one * first_rows + (1.0 - beta_one) * gradient
    second_next = beta_two * second_rows + (1.0 - beta_two) * gradient * gradient
    step_size = first_next / correction_one / (jnp.sqrt(second_next / correction_two) + epsilon)
    updated = (
        weight_rows.astype(jnp.float32) * (1.0 - learn_rate * decay_rate) - learn_rate * step_size
    ).astype(jnp.bfloat16)
    return updated, first_next, second_next


def adam_kernel(owner_ref, moments_ref, weight_ref, *refs):
    part_refs, (new_ref, first_ref, second_ref, gradient, inverse_ref) = refs[:-5], refs[-5:]
    for slot in range(moments_ref.shape[0]):
        inverse_ref[owner_ref[slot]] = slot
    total = part_refs[0][0].astype(jnp.float32)
    for part_ref in part_refs[1:]:
        total = total + part_ref[0].astype(jnp.float32)
    gradient[...] = total.T
    for pair in range(moments_ref.shape[0] // 2):
        even = moments_ref[inverse_ref[2 * pair]].astype(jnp.float32)
        odd = moments_ref[inverse_ref[2 * pair + 1]].astype(jnp.float32)
        rows = pl.ds(pair * 2 * SUB, 2 * SUB)
        new_ref[rows, :], first_ref[rows, :], second_ref[rows, :] = adam(
            weight_ref[rows, :],
            jnp.concatenate([even[:SUB], odd[:SUB]], axis=0),
            jnp.concatenate([even[SUB:], odd[SUB:]], axis=0),
            gradient[rows, :],
        )


def adam_rows(parts, moments, weight_rows, owners):
    row_block, width = weight_rows.shape
    whole = pl.BlockSpec((row_block, width), lambda i, *_: (0, 0))
    return pl.pallas_call(
        adam_kernel,
        grid_spec=pltpu.PrefetchScalarGridSpec(
            num_scalar_prefetch=1,
            grid=(1,),
            in_specs=[pl.BlockSpec(moments.shape, lambda i, *_: (0, 0, 0)), whole]
            + [pl.BlockSpec((1, width, row_block), lambda i, *_: (0, 0, 0))] * len(parts),
            out_specs=[whole] * 3,
            scratch_shapes=[
                pltpu.VMEM((row_block, width), jnp.float32),
                pltpu.SMEM((moments.shape[0],), jnp.int32),
            ],
        ),
        out_shape=[
            jax.ShapeDtypeStruct((row_block, width), jnp.bfloat16),
            jax.ShapeDtypeStruct((row_block, width), jnp.float32),
            jax.ShapeDtypeStruct((row_block, width), jnp.float32),
        ],
        compiler_params=pltpu.CompilerParams(vmem_limit_bytes=12 * MIB),
        cost_estimate=cost(20 * row_block * width, 16 * row_block * width),
        name="adam_rows",
    )(owners, moments, weight_rows, *parts)


class Grid:
    def __init__(self, groups, shards):
        self.shards = shards
        self.cores = 2 if groups % 2 == 0 else 1
        self.minor = 2 if shards % 2 == 0 else 1
        self.outer = groups // self.cores
        self.far = shards // self.minor
        self.swaps = self.cores == 2 and self.minor == self.outer
        self.near, self.side = self.minor, self.outer

    def moved(self, position, core=0, near=0, side=0, far=0):
        group, shard = position // self.shards, position % self.shards
        outer, on = group // self.cores, (group % self.cores + core) % self.cores
        depth, minor = shard // self.minor, shard % self.minor
        swapped = on if self.swaps else 0
        minor = (minor + near + (side - near) * swapped) % self.minor
        outer = (outer + side + (near - side) * swapped) % self.outer
        depth = (depth + far) % self.far
        return (outer * self.cores + on) * self.shards + depth * self.minor + minor

    def send(self, value, **steps):
        devices = self.outer * self.cores * self.shards
        pairs = [(p, self.moved(p, **steps)) for p in range(devices)]
        return lax.ppermute(value, AXES, pairs)


def sum_kernel(start, count, terms, *refs):
    out_ref = refs[-1]
    total = refs[0][start : start + count].astype(jnp.float32)
    for ref in refs[1:terms]:
        total = total + ref[start : start + count].astype(jnp.float32)
    out_ref[...] = total.astype(out_ref.dtype)


def rounded_sum(terms, start, count, after=()):
    shape = (count, *terms[0].shape[1:])
    if shape[-1] % 128:
        total = sum(term[start : start + count].astype(jnp.float32) for term in terms)
        return total.astype(terms[0].dtype)
    whole = pl.BlockSpec(memory_space=pltpu.VMEM)
    size = count * shape[1] * shape[2]
    return pl.pallas_call(
        functools.partial(sum_kernel, start, count, len(terms)),
        in_specs=[whole] * len(terms) + [pl.BlockSpec(memory_space=pl.ANY)] * len(after),
        out_specs=whole,
        out_shape=jax.ShapeDtypeStruct(shape, terms[0].dtype),
        compiler_params=pltpu.CompilerParams(vmem_limit_bytes=12 * MIB),
        cost_estimate=cost(size * len(terms), 2 * size * (len(terms) + 1)),
        name="add_blocks",
    )(*terms, *after)


def sum_chunks(grid):
    half = (grid.far + 1) // 2
    return [part for part in (range(half), range(half, grid.far)) if part]


def shard_chunks(grid):
    return [part for part in (range(1), range(1, grid.far)) if part]


def tables(grid, devices):
    sums = [
        dict(core=core, near=near, side=side, far=far)
        for chunk in sum_chunks(grid)
        for core in range(grid.cores)
        for near in [*range(1, grid.near), 0]
        for side in range(grid.side)
        for far in chunk
    ]
    shards = [
        dict(core=-core, near=-near, side=-side, far=-far)
        for chunk in shard_chunks(grid)
        for core in range(grid.cores)
        for near in range(grid.near)
        for side in range(grid.side)
        for far in chunk
    ]
    return np.array(
        [[grid.moved(p, **step) for step in sums + shards] for p in range(devices)], np.int32
    )


def reduce_rows(grid, blocks_of, project_now):
    plan = []
    start = 0
    for number, chunk in enumerate(sum_chunks(grid)):
        plan.insert(0, (number, chunk, start))
        start += len(chunk)
    addends = {}
    if grid.cores > 1:
        for number, chunk, start in plan:
            block = blocks_of(1, number, start, len(chunk), None, False)[0]
            addends[number] = grid.send(block, core=1)
    held = {}
    for number, chunk, start in plan:
        parts = blocks_of(0, number, start, len(chunk), addends.get(number), True)
        held[number] = [parts[-1]]
        for step, part in enumerate(parts[:-1], 1):
            held[number].append(grid.send(part, near=step))
    projection = project_now()
    last = []
    for number, chunk, _ in plan:
        count = len(chunk)
        kept = held[number]
        ends = list(kept)
        for step in range(1, grid.side):
            part = rounded_sum(kept, step * count, count)
            ends.append(grid.send(part, side=step))
        held[number] = ends
    for number, chunk, _ in plan:
        ends = held[number]
        for index, far in enumerate(chunk):
            if not far:
                last.extend(ends)
                continue
            last.append(grid.send(rounded_sum(ends, index, 1), far=far))
    return last, projection


def gather_shards(grid, own):
    arrived = {far: grid.send(own, far=far) for far in range(1, grid.far)}
    arrived[0] = own
    pieces, marks = [], []
    for chunk in shard_chunks(grid):
        base = joined([arrived[far] for far in chunk])
        both = [base] + [grid.send(base, side=step) for step in range(1, grid.side)]
        nears = [grid.send(part, near=step) for step in range(1, grid.near) for part in both]
        marks.append((both[1:], nears, [arrived[far] for far in chunk]))
        pieces += both + nears
        for core in range(1, grid.cores):
            pieces += [grid.send(part, core=core) for part in both + nears]
    return pieces, marks


def joined(arrays):
    return arrays[0] if len(arrays) == 1 else jnp.concatenate(arrays, axis=0)


def body(tokens, cotangent, old_weight, old_first, old_second, old_owner, new_owner):
    devices = lax.axis_size(AXES)
    groups = lax.axis_size("rep")
    shards = lax.axis_size("fsdp")
    features = tokens.shape[1]
    row_block, width = old_weight.shape
    strip = row_block * width // devices
    grid = Grid(groups, shards)
    me = lax.axis_index(AXES)
    by_tile = row_block == devices * SUB and width % 128 == 0 and devices % 2 == 0

    row = lax.dynamic_index_in_dim(jnp.asarray(tables(grid, devices)), me, 0, keepdims=False)
    per_far = grid.near * grid.side
    own = (grid.near - 1) * grid.side * len(sum_chunks(grid)[0])

    pieces, marks = gather_shards(grid, old_weight[None])
    if by_tile:
        packed = pack_moments(old_first, old_second, new_owner, groups)
    else:
        slot_ids = jnp.arange(devices, dtype=jnp.int32)
        placing = jnp.take(new_owner, slot_ids % shards) * groups + slot_ids // shards
        both = jnp.stack([old_first, old_second]).astype(jnp.bfloat16)
        packed = jnp.take(
            jnp.transpose(both.reshape(2, devices, strip), (1, 0, 2)), placing, axis=0
        )
    arrived = lax.all_to_all(packed, AXES, split_axis=0, concat_axis=0, tiled=True)

    turned = cotangent.T

    waits = {
        (1, 1): [packed, *marks[0][0]],
        (1, 0): [marks[-1][2][0], marks[-1][2][-1]],
        (0, 1): [*marks[-1][2], *marks[0][1]],
        (0, 0): [*marks[-1][0], marks[-1][1][0]],
    }
    if not by_tile:
        waits = {}
    done = []

    def blocks_of(core, chunk, start, count, addend, cut):
        first = (start * grid.cores + core * count) * per_far
        per_step = grid.side * count
        after = [*waits.get((core, chunk), ()), *done[-1:]]
        blocks = grad_blocks(
            tokens, turned, row, new_owner, first, grid.near, per_step, addend, cut, after
        )
        done.append(blocks[0])
        return blocks

    def project_now():
        if by_tile:
            return project(tokens, pieces, row, devices, own, old_owner, new_owner)
        return ()

    parts, projection = reduce_rows(grid, blocks_of, project_now)
    if by_tile:
        projected, weight_rows = projection
        return (projected, *adam_rows(parts, arrived, weight_rows, old_owner))
    inverse = jnp.zeros((devices,), jnp.int32).at[old_owner].set(slot_ids)
    held = jnp.zeros((devices, devices, strip), jnp.bfloat16)
    held = held.at[jnp.take(old_owner, row[devices:])].set(
        joined(pieces).reshape(devices, devices, strip)
    )
    logical = jnp.transpose(held, (1, 0, 2)).reshape(features, width)
    projected = jnp.dot(tokens, logical, preferred_element_type=jnp.float32).astype(jnp.bfloat16)
    own_block = jnp.take(placing, me)
    weight_rows = lax.dynamic_slice_in_dim(logical, own_block * row_block, row_block, 0)
    moved = jnp.transpose(jnp.take(arrived, inverse, axis=0), (1, 0, 2))
    first_rows, second_rows = moved.astype(jnp.float32).reshape(2, row_block, width)
    gradient = sum(part[0].astype(jnp.float32) for part in parts).T
    return (projected, *adam(weight_rows, first_rows, second_rows, gradient))


def solution(mesh):
    placed = P(AXES, None)
    return jax.shard_map(
        body,
        mesh=mesh,
        in_specs=(placed,) * 5 + (P(), P()),
        out_specs=(placed,) * 4,
        check_vma=False,
    )
```

```python
import functools
import jax
import jax.numpy as jnp
import numpy as np
from jax import lax
from jax.experimental import pallas as pl
from jax.experimental.pallas import tpu as pltpu
from jax.sharding import PartitionSpec as P

beta_one = 0.9
beta_two = 0.95
learn_rate = 0.001
decay_rate = 0.1
epsilon = 1e-08
correction_one = 1.0 - 0.9**10
correction_two = 1.0 - 0.95**10

AXES = ("rep", "fsdp")
MIB = 1024 * 1024
COLUMNS = 2
SUB = 8


def cost(flops, moved):
    return pl.CostEstimate(flops=flops, bytes_accessed=moved, transcendentals=0)


def block_at(new_ref, groups, position):
    shards = new_ref.shape[0]
    return new_ref[lax.rem(position, shards)] * groups + lax.div(position, shards)


def grad_kernel(per_step, adds, outs, row_ref, new_ref, *refs):
    token_refs, turned_ref, refs = refs[:per_step], refs[per_step], refs[per_step + 1 :]
    out_refs = refs[-outs:]

    def write(out_ref):
        for slot, token_ref in enumerate(token_refs):
            block = jnp.dot(turned_ref[...], token_ref[...], preferred_element_type=jnp.float32)
            if adds:
                block = block + refs[0][slot].astype(jnp.float32)
            out_ref[slot] = block.astype(out_ref.dtype)

    if outs == 1:
        write(out_refs[0])
        return
    for part, out_ref in enumerate(out_refs):
        pl.when(pl.program_id(0) == part)(functools.partial(write, out_ref))


def grad_blocks(
    tokens, turned, row, new_owner, first, steps, per_step, addend=None, cut=False, after=()
):
    rows, features = tokens.shape
    width = turned.shape[0]
    blocks = steps * per_step
    groups = lax.axis_size("rep")
    row_block = features // (groups * new_owner.shape[0])
    if row_block % 128:
        chosen = row[first : first + blocks]
        chosen = jnp.take(new_owner, chosen % new_owner.shape[0]) * groups + (
            chosen // new_owner.shape[0]
        )
        whole = jnp.dot(turned, tokens, preferred_element_type=jnp.float32)
        parts = jnp.transpose(whole.reshape(width, features // row_block, row_block), (1, 0, 2))
        parts = jnp.take(parts, chosen, axis=0)
        if addend is not None:
            parts = parts + addend.astype(jnp.float32)
        parts = parts.astype(jnp.bfloat16)
        return list(jnp.split(parts, steps)) if cut else [parts]

    def token_map(slot):
        return lambda i, row_ref, new_ref: (
            0,
            block_at(new_ref, groups, row_ref[first + i * per_step + slot]),
        )

    block = pl.BlockSpec((per_step, width, row_block), lambda i, *_: (i, 0, 0))
    fixed = pl.BlockSpec((per_step, width, row_block), lambda i, *_: (0, 0, 0))
    added = [] if addend is None else [addend]
    outs = steps if cut else 1
    return pl.pallas_call(
        functools.partial(grad_kernel, per_step, len(added), outs),
        grid_spec=pltpu.PrefetchScalarGridSpec(
            num_scalar_prefetch=2,
            grid=(steps,),
            in_specs=[pl.BlockSpec((rows, row_block), token_map(s)) for s in range(per_step)]
            + [pl.BlockSpec((width, rows), lambda i, *_: (0, 0))]
            + [block] * len(added)
            + [pl.BlockSpec(memory_space=pl.ANY)] * len(after),
            out_specs=[fixed if cut else block] * outs,
        ),
        out_shape=[jax.ShapeDtypeStruct((blocks // outs, width, row_block), jnp.bfloat16)] * outs,
        compiler_params=pltpu.CompilerParams(vmem_limit_bytes=46 * MIB),
        cost_estimate=cost(
            2 * rows * width * blocks * row_block,
            2 * blocks * row_block * (rows + width * (1 + len(added))) + 2 * rows * width,
        ),
        name="weight_gradient",
    )(row, new_owner, *([tokens] * per_step), turned, *added, *after)


def pack_kernel(groups, new_ref, first_ref, second_ref, out_ref):
    for slot in range(out_ref.shape[0]):
        block = block_at(new_ref, groups, slot)
        rows = pl.ds(pl.multiple_of(block * SUB, SUB), SUB)
        pair = jnp.concatenate([first_ref[rows, :], second_ref[rows, :]], axis=0)
        out_ref[slot] = pair.astype(out_ref.dtype)


def pack_moments(first, second, new_owner, groups):
    devices = new_owner.shape[0] * groups
    width = first.shape[1]
    return pl.pallas_call(
        functools.partial(pack_kernel, groups),
        in_specs=[
            pl.BlockSpec(memory_space=pltpu.SMEM),
            pl.BlockSpec(memory_space=pltpu.VMEM),
            pl.BlockSpec(memory_space=pltpu.VMEM),
        ],
        out_specs=pl.BlockSpec(memory_space=pltpu.VMEM),
        out_shape=jax.ShapeDtypeStruct((devices, 2 * SUB, width), jnp.bfloat16),
        cost_estimate=cost(0, 12 * first.size),
        name="pack_moments",
    )(new_owner, first, second)


def project_kernel(groups, first, own, count, row_ref, old_ref, new_ref, token_ref, *refs):
    piece_refs, (out_ref, rows_ref, held, logical, sems) = refs[:count], refs[-5:]
    devices, row_block, _ = held.shape

    @pl.when(pl.program_id(0) == 0)
    def _():
        copies = []
        for piece_ref in piece_refs:
            for index in range(piece_ref.shape[0]):
                slot = len(copies)
                target = held.at[old_ref[row_ref[first + slot]]]
                copies.append(pltpu.make_async_copy(piece_ref.at[index], target, sems.at[slot]))
        for copy in copies:
            copy.start()
        for copy in copies:
            copy.wait()

        def place(pair, carry):
            for block in range(0, devices, 2):
                span = pl.ds(block * SUB, 2 * SUB)
                top = held[2 * pair, span, :]
                low = held[2 * pair + 1, span, :]
                for half in range(2):
                    part = slice(half * SUB, (half + 1) * SUB)
                    start = (block + half) * row_block + pair * 2 * SUB
                    logical[pl.ds(pl.multiple_of(start, 2 * SUB), 2 * SUB), :] = jnp.concatenate(
                        [top[part], low[part]], axis=0
                    )
            return carry

        lax.fori_loop(0, devices // 2, place, 0)
        start = block_at(new_ref, groups, row_ref[own]) * row_block
        start = pl.multiple_of(start, row_block)
        rows_ref[...] = logical[pl.ds(start, row_block), :]

    out_ref[...] = jnp.dot(
        token_ref[...], logical[...], preferred_element_type=jnp.float32
    ).astype(out_ref.dtype)


def project(tokens, pieces, row, first, own, old_owner, new_owner, part, parts, before):
    rows, features = tokens.shape
    _, row_block, width = pieces[0].shape
    before = [] if before is None else [before]
    devices = old_owner.shape[0]
    tile = rows // 4
    return pl.pallas_call(
        functools.partial(
            project_kernel, devices // new_owner.shape[0], first, own, len(pieces)
        ),
        grid_spec=pltpu.PrefetchScalarGridSpec(
            num_scalar_prefetch=3,
            grid=(rows // tile,),
            in_specs=[pl.BlockSpec((tile, features), lambda i, *_: (i, 0))]
            + [pl.BlockSpec(memory_space=pl.ANY)] * (len(pieces) + len(before)),
            out_specs=[
                pl.BlockSpec((tile, width), lambda i, *_: (i, part)),
                pl.BlockSpec((row_block, width), lambda i, *_: (0, 0)),
            ],
            scratch_shapes=[
                pltpu.VMEM((devices, row_block, width), jnp.bfloat16),
                pltpu.VMEM((features, width), jnp.bfloat16),
                pltpu.SemaphoreType.DMA((devices,)),
            ],
        ),
        out_shape=[
            jax.ShapeDtypeStruct((rows, parts * width), jnp.bfloat16),
            jax.ShapeDtypeStruct((row_block, width), jnp.bfloat16),
        ],
        input_output_aliases={4 + len(pieces): 0} if before else {},
        compiler_params=pltpu.CompilerParams(vmem_limit_bytes=46 * MIB),
        cost_estimate=cost(
            2 * rows * width * features, 2 * (rows * features + features * width + rows * width)
        ),
        name="project",
    )(row, old_owner, new_owner, tokens, *pieces, *before)


def adam(weight_rows, first_rows, second_rows, gradient):
    first_next = beta_one * first_rows + (1.0 - beta_one) * gradient
    second_next = beta_two * second_rows + (1.0 - beta_two) * gradient * gradient
    step_size = first_next / correction_one / (jnp.sqrt(second_next / correction_two) + epsilon)
    updated = (
        weight_rows.astype(jnp.float32) * (1.0 - learn_rate * decay_rate) - learn_rate * step_size
    ).astype(jnp.bfloat16)
    return updated, first_next, second_next


def adam_kernel(columns, owner_ref, moments_ref, *refs):
    weight_refs, refs = refs[:columns], refs[columns:]
    part_refs, (new_ref, first_ref, second_ref, gradient, inverse_ref) = refs[:-5], refs[-5:]
    for slot in range(moments_ref.shape[0]):
        inverse_ref[owner_ref[slot]] = slot
    total = part_refs[0][0].astype(jnp.float32)
    for part_ref in part_refs[1:]:
        total = total + part_ref[0].astype(jnp.float32)
    gradient[...] = total.T
    for pair in range(moments_ref.shape[0] // 2):
        even = moments_ref[inverse_ref[2 * pair]].astype(jnp.float32)
        odd = moments_ref[inverse_ref[2 * pair + 1]].astype(jnp.float32)
        rows = pl.ds(pair * 2 * SUB, 2 * SUB)
        new_ref[rows, :], first_ref[rows, :], second_ref[rows, :] = adam(
            jnp.concatenate([ref[rows, :] for ref in weight_refs], axis=1),
            jnp.concatenate([even[:SUB], odd[:SUB]], axis=0),
            jnp.concatenate([even[SUB:], odd[SUB:]], axis=0),
            gradient[rows, :],
        )


def adam_rows(parts, moments, weight_rows, owners):
    row_block, columns = weight_rows[0].shape
    width = columns * len(weight_rows)
    whole = pl.BlockSpec((row_block, width), lambda i, *_: (0, 0))
    return pl.pallas_call(
        functools.partial(adam_kernel, len(weight_rows)),
        grid_spec=pltpu.PrefetchScalarGridSpec(
            num_scalar_prefetch=1,
            grid=(1,),
            in_specs=[pl.BlockSpec(moments.shape, lambda i, *_: (0, 0, 0))]
            + [pl.BlockSpec((row_block, columns), lambda i, *_: (0, 0))] * len(weight_rows)
            + [pl.BlockSpec((1, width, row_block), lambda i, *_: (0, 0, 0))] * len(parts),
            out_specs=[whole] * 3,
            scratch_shapes=[
                pltpu.VMEM((row_block, width), jnp.float32),
                pltpu.SMEM((moments.shape[0],), jnp.int32),
            ],
        ),
        out_shape=[
            jax.ShapeDtypeStruct((row_block, width), jnp.bfloat16),
            jax.ShapeDtypeStruct((row_block, width), jnp.float32),
            jax.ShapeDtypeStruct((row_block, width), jnp.float32),
        ],
        compiler_params=pltpu.CompilerParams(vmem_limit_bytes=12 * MIB),
        cost_estimate=cost(20 * row_block * width, 16 * row_block * width),
        name="adam_rows",
    )(owners, moments, *weight_rows, *parts)


class Grid:
    def __init__(self, groups, shards):
        self.shards = shards
        self.cores = 2 if groups % 2 == 0 else 1
        self.minor = 2 if shards % 2 == 0 else 1
        self.outer = groups // self.cores
        self.far = shards // self.minor
        self.swaps = self.cores == 2 and self.minor == self.outer
        self.near, self.side = self.minor, self.outer

    def moved(self, position, core=0, near=0, side=0, far=0):
        group, shard = position // self.shards, position % self.shards
        outer, on = group // self.cores, (group % self.cores + core) % self.cores
        depth, minor = shard // self.minor, shard % self.minor
        swapped = on if self.swaps else 0
        minor = (minor + near + (side - near) * swapped) % self.minor
        outer = (outer + side + (near - side) * swapped) % self.outer
        depth = (depth + far) % self.far
        return (outer * self.cores + on) * self.shards + depth * self.minor + minor

    def send(self, value, **steps):
        devices = self.outer * self.cores * self.shards
        pairs = [(p, self.moved(p, **steps)) for p in range(devices)]
        return lax.ppermute(value, AXES, pairs)


def rounded_sum(terms, start, count):
    total = sum(term[start : start + count].astype(jnp.float32) for term in terms)
    return total.astype(terms[0].dtype)


def sum_chunks(grid):
    half = grid.far // 2
    return [sorted({d, (grid.far - d) % grid.far}) for d in range(half + 1)]


def shard_chunks(grid):
    return [list(range(grid.far))]


def tables(grid, devices):
    sums = [
        dict(core=core, near=near, side=side, far=far)
        for chunk in sum_chunks(grid)
        for core in range(grid.cores)
        for near in [*range(1, grid.near), 0]
        for side in range(grid.side)
        for far in chunk
    ]
    shards = [
        dict(core=-core, near=-near, side=-side, far=-far)
        for chunk in shard_chunks(grid)
        for core in range(grid.cores)
        for near in range(grid.near)
        for side in range(grid.side)
        for far in chunk
    ]
    return np.array(
        [[grid.moved(p, **step) for step in sums + shards] for p in range(devices)], np.int32
    )


def reduce_rows(grid, blocks_of, project_now):
    plan = []
    start = 0
    for number, chunk in enumerate(sum_chunks(grid)):
        plan.insert(0, (number, chunk, start))
        start += len(chunk)
    addends = {}
    if grid.cores > 1:
        for number, chunk, start in plan:
            block = blocks_of(1, number, start, len(chunk), None, False)[0]
            addends[number] = grid.send(block, core=1)
    held = {}
    for number, chunk, start in plan:
        parts = blocks_of(0, number, start, len(chunk), addends.get(number), True)
        held[number] = [parts[-1]]
        for step, part in enumerate(parts[:-1], 1):
            held[number].append(grid.send(part, near=step))
    projection = project_now()
    last = []
    for number, chunk, _ in plan:
        count = len(chunk)
        kept = held[number]
        ends = list(kept)
        for step in range(1, grid.side):
            part = rounded_sum(kept, step * count, count)
            ends.append(grid.send(part, side=step))
        held[number] = ends
    for number, chunk, _ in plan:
        ends = held[number]
        for index, far in enumerate(chunk):
            if not far:
                last.extend(ends)
                continue
            last.append(grid.send(rounded_sum(ends, index, 1), far=far))
    return last, projection


def gather_shards(grid, own):
    arrived = {far: grid.send(own, far=far) for far in range(1, grid.far)}
    arrived[0] = own
    pieces, marks = [], []
    for chunk in shard_chunks(grid):
        base = joined([arrived[far] for far in chunk])
        sides = [grid.send(base, side=step) for step in range(1, grid.side)]
        both = [joined([base] + sides)]
        nears = [grid.send(part, near=step) for step in range(1, grid.near) for part in both]
        marks.append((sides, nears, [arrived[far] for far in chunk]))
        pieces += both + nears
        for core in range(1, grid.cores):
            pieces += [grid.send(part, core=core) for part in both + nears]
    return pieces, marks


def joined(arrays):
    return arrays[0] if len(arrays) == 1 else jnp.concatenate(arrays, axis=0)


def body(tokens, cotangent, old_weight, old_first, old_second, old_owner, new_owner):
    devices = lax.axis_size(AXES)
    groups = lax.axis_size("rep")
    shards = lax.axis_size("fsdp")
    features = tokens.shape[1]
    row_block, width = old_weight.shape
    strip = row_block * width // devices
    grid = Grid(groups, shards)
    me = lax.axis_index(AXES)
    by_tile = row_block == devices * SUB and width % 128 == 0 and devices % 2 == 0

    row = lax.dynamic_index_in_dim(jnp.asarray(tables(grid, devices)), me, 0, keepdims=False)
    per_far = grid.near * grid.side
    own = (grid.near - 1) * grid.side * len(sum_chunks(grid)[0])

    cuts = COLUMNS if by_tile and width % (128 * COLUMNS) == 0 else 1
    gathered = [gather_shards(grid, part[None]) for part in jnp.split(old_weight, cuts, axis=1)]
    marks = [mark for _, part in gathered for mark in part]
    if by_tile:
        packed = pack_moments(old_first, old_second, new_owner, groups)
    else:
        slot_ids = jnp.arange(devices, dtype=jnp.int32)
        placing = jnp.take(new_owner, slot_ids % shards) * groups + slot_ids // shards
        both = jnp.stack([old_first, old_second]).astype(jnp.bfloat16)
        packed = jnp.take(
            jnp.transpose(both.reshape(2, devices, strip), (1, 0, 2)), placing, axis=0
        )
    arrived = lax.all_to_all(packed, AXES, split_axis=0, concat_axis=0, tiled=True)

    turned = cotangent.T

    waits = {}
    if not by_tile:
        waits = {}
    done = []

    def blocks_of(core, chunk, start, count, addend, cut):
        first = (start * grid.cores + core * count) * per_far
        per_step = grid.side * count
        after = [*waits.get((core, chunk), ()), *done[-1:]]
        blocks = grad_blocks(
            tokens, turned, row, new_owner, first, grid.near, per_step, addend, cut, after
        )
        done.append(blocks[0])
        return blocks

    def project_now():
        if not by_tile:
            return ()
        projected, weight_rows = None, []
        for part, (pieces, _) in enumerate(gathered):
            projected, rows = project(
                tokens, pieces, row, devices, own, old_owner, new_owner, part, cuts, projected
            )
            weight_rows.append(rows)
        return projected, weight_rows

    parts, projection = reduce_rows(grid, blocks_of, project_now)
    if by_tile:
        projected, weight_rows = projection
        return (projected, *adam_rows(parts, arrived, weight_rows, old_owner))
    inverse = jnp.zeros((devices,), jnp.int32).at[old_owner].set(slot_ids)
    held = jnp.zeros((devices, devices, strip), jnp.bfloat16)
    held = held.at[jnp.take(old_owner, row[devices:])].set(
        joined(gathered[0][0]).reshape(devices, devices, strip)
    )
    logical = jnp.transpose(held, (1, 0, 2)).reshape(features, width)
    projected = jnp.dot(tokens, logical, preferred_element_type=jnp.float32).astype(jnp.bfloat16)
    own_block = jnp.take(placing, me)
    weight_rows = lax.dynamic_slice_in_dim(logical, own_block * row_block, row_block, 0)
    moved = jnp.transpose(jnp.take(arrived, inverse, axis=0), (1, 0, 2))
    first_rows, second_rows = moved.astype(jnp.float32).reshape(2, row_block, width)
    gradient = sum(part[0].astype(jnp.float32) for part in parts).T
    return (projected, *adam(weight_rows, first_rows, second_rows, gradient))


def solution(mesh):
    placed = P(AXES, None)
    return jax.shard_map(
        body,
        mesh=mesh,
        in_specs=(placed,) * 5 + (P(), P()),
        out_specs=(placed,) * 4,
        check_vma=False,
    )
```

```python
import functools
import jax
import jax.numpy as jnp
import numpy as np
from jax import lax
from jax.experimental import pallas as pl
from jax.experimental.pallas import tpu as pltpu
from jax.sharding import PartitionSpec as P

beta_one = 0.9
beta_two = 0.95
learn_rate = 0.001
decay_rate = 0.1
epsilon = 1e-08
correction_one = 1.0 - 0.9**10
correction_two = 1.0 - 0.95**10

AXES = ("rep", "fsdp")
MIB = 1024 * 1024
COLUMNS = 1
SUB = 8


def cost(flops, moved):
    return pl.CostEstimate(flops=flops, bytes_accessed=moved, transcendentals=0)


def block_at(new_ref, groups, position):
    shards = new_ref.shape[0]
    return new_ref[lax.rem(position, shards)] * groups + lax.div(position, shards)


def grad_kernel(per_step, adds, outs, row_ref, new_ref, *refs):
    token_refs, turned_ref, refs = refs[:per_step], refs[per_step], refs[per_step + 1 :]
    out_refs = refs[-outs:]

    def write(out_ref):
        for slot, token_ref in enumerate(token_refs):
            block = jnp.dot(turned_ref[...], token_ref[...], preferred_element_type=jnp.float32)
            if adds:
                block = block + refs[0][slot].astype(jnp.float32)
            out_ref[slot] = block.astype(out_ref.dtype)

    if outs == 1:
        write(out_refs[0])
        return
    for part, out_ref in enumerate(out_refs):
        pl.when(pl.program_id(0) == part)(functools.partial(write, out_ref))


def grad_blocks(
    tokens, turned, row, new_owner, first, steps, per_step, addend=None, cut=False, after=()
):
    rows, features = tokens.shape
    width = turned.shape[0]
    blocks = steps * per_step
    groups = lax.axis_size("rep")
    row_block = features // (groups * new_owner.shape[0])
    if row_block % 128:
        chosen = row[first : first + blocks]
        chosen = jnp.take(new_owner, chosen % new_owner.shape[0]) * groups + (
            chosen // new_owner.shape[0]
        )
        whole = jnp.dot(turned, tokens, preferred_element_type=jnp.float32)
        parts = jnp.transpose(whole.reshape(width, features // row_block, row_block), (1, 0, 2))
        parts = jnp.take(parts, chosen, axis=0)
        if addend is not None:
            parts = parts + addend.astype(jnp.float32)
        parts = parts.astype(jnp.bfloat16)
        return list(jnp.split(parts, steps)) if cut else [parts]

    def token_map(slot):
        return lambda i, row_ref, new_ref: (
            0,
            block_at(new_ref, groups, row_ref[first + i * per_step + slot]),
        )

    block = pl.BlockSpec((per_step, width, row_block), lambda i, *_: (i, 0, 0))
    fixed = pl.BlockSpec((per_step, width, row_block), lambda i, *_: (0, 0, 0))
    added = [] if addend is None else [addend]
    outs = steps if cut else 1
    return pl.pallas_call(
        functools.partial(grad_kernel, per_step, len(added), outs),
        grid_spec=pltpu.PrefetchScalarGridSpec(
            num_scalar_prefetch=2,
            grid=(steps,),
            in_specs=[pl.BlockSpec((rows, row_block), token_map(s)) for s in range(per_step)]
            + [pl.BlockSpec((width, rows), lambda i, *_: (0, 0))]
            + [block] * len(added)
            + [pl.BlockSpec(memory_space=pl.ANY)] * len(after),
            out_specs=[fixed if cut else block] * outs,
        ),
        out_shape=[jax.ShapeDtypeStruct((blocks // outs, width, row_block), jnp.bfloat16)] * outs,
        compiler_params=pltpu.CompilerParams(vmem_limit_bytes=46 * MIB),
        cost_estimate=cost(
            2 * rows * width * blocks * row_block,
            2 * blocks * row_block * (rows + width * (1 + len(added))) + 2 * rows * width,
        ),
        name="weight_gradient",
    )(row, new_owner, *([tokens] * per_step), turned, *added, *after)


def pack_kernel(groups, new_ref, first_ref, second_ref, out_ref):
    for slot in range(out_ref.shape[0]):
        block = block_at(new_ref, groups, slot)
        rows = pl.ds(pl.multiple_of(block * SUB, SUB), SUB)
        pair = jnp.concatenate([first_ref[rows, :], second_ref[rows, :]], axis=0)
        out_ref[slot] = pair.astype(out_ref.dtype)


def pack_moments(first, second, new_owner, groups):
    devices = new_owner.shape[0] * groups
    width = first.shape[1]
    return pl.pallas_call(
        functools.partial(pack_kernel, groups),
        in_specs=[
            pl.BlockSpec(memory_space=pltpu.SMEM),
            pl.BlockSpec(memory_space=pltpu.VMEM),
            pl.BlockSpec(memory_space=pltpu.VMEM),
        ],
        out_specs=pl.BlockSpec(memory_space=pltpu.VMEM),
        out_shape=jax.ShapeDtypeStruct((devices, 2 * SUB, width), jnp.bfloat16),
        cost_estimate=cost(0, 12 * first.size),
        name="pack_moments",
    )(new_owner, first, second)


def project_kernel(groups, first, own, count, row_ref, old_ref, new_ref, token_ref, *refs):
    piece_refs, (out_ref, rows_ref, held, logical, total, sems) = refs[:count], refs[-6:]
    devices, row_block, _ = held.shape
    step = pl.program_id(0)
    blocks = logical.shape[0] // row_block

    @pl.when(step == 0)
    def _():
        copies = []
        for piece_ref in piece_refs:
            for index in range(piece_ref.shape[0]):
                slot = len(copies)
                target = held.at[old_ref[row_ref[first + slot]]]
                copies.append(pltpu.make_async_copy(piece_ref.at[index], target, sems.at[slot]))
        for copy in copies:
            copy.start()
        total[...] = jnp.zeros_like(total)
        for copy in copies:
            copy.wait()

    for pair in range(devices // 2):
        for block in range(0, blocks, 2):
            span = pl.ds(pl.multiple_of((step * blocks + block) * SUB, 2 * SUB), 2 * SUB)
            top = held[2 * pair, span, :]
            low = held[2 * pair + 1, span, :]
            for half in range(2):
                part = slice(half * SUB, (half + 1) * SUB)
                start = (block + half) * row_block + pair * 2 * SUB
                logical[start : start + 2 * SUB, :] = jnp.concatenate(
                    [top[part], low[part]], axis=0
                )

    block = block_at(new_ref, groups, row_ref[own])

    @pl.when(lax.div(block, blocks) == step)
    def _():
        start = pl.multiple_of(lax.rem(block, blocks) * row_block, row_block)
        rows_ref[...] = logical[pl.ds(start, row_block), :]

    total[...] += jnp.dot(token_ref[...], logical[...], preferred_element_type=jnp.float32)

    @pl.when(step == pl.num_programs(0) - 1)
    def _():
        out_ref[...] = total[...].astype(out_ref.dtype)


def project(tokens, pieces, row, first, own, old_owner, new_owner, part, parts, before):
    rows, features = tokens.shape
    _, row_block, width = pieces[0].shape
    before = [] if before is None else [before]
    devices = old_owner.shape[0]
    tile = 4 * row_block
    return pl.pallas_call(
        functools.partial(
            project_kernel, devices // new_owner.shape[0], first, own, len(pieces)
        ),
        grid_spec=pltpu.PrefetchScalarGridSpec(
            num_scalar_prefetch=3,
            grid=(features // tile,),
            in_specs=[pl.BlockSpec((rows, tile), lambda i, *_: (0, i))]
            + [pl.BlockSpec(memory_space=pl.ANY)] * (len(pieces) + len(before)),
            out_specs=[
                pl.BlockSpec((rows, width), lambda i, *_: (0, part)),
                pl.BlockSpec((row_block, width), lambda i, *_: (0, 0)),
            ],
            scratch_shapes=[
                pltpu.VMEM((devices, row_block, width), jnp.bfloat16),
                pltpu.VMEM((tile, width), jnp.bfloat16),
                pltpu.VMEM((rows, width), jnp.float32),
                pltpu.SemaphoreType.DMA((devices,)),
            ],
        ),
        out_shape=[
            jax.ShapeDtypeStruct((rows, parts * width), jnp.bfloat16),
            jax.ShapeDtypeStruct((row_block, width), jnp.bfloat16),
        ],
        input_output_aliases={4 + len(pieces): 0} if before else {},
        compiler_params=pltpu.CompilerParams(vmem_limit_bytes=46 * MIB),
        cost_estimate=cost(
            2 * rows * width * features, 2 * (rows * features + features * width + rows * width)
        ),
        name="project",
    )(row, old_owner, new_owner, tokens, *pieces, *before)


def adam(weight_rows, first_rows, second_rows, gradient):
    first_next = beta_one * first_rows + (1.0 - beta_one) * gradient
    second_next = beta_two * second_rows + (1.0 - beta_two) * gradient * gradient
    step_size = first_next / correction_one / (jnp.sqrt(second_next / correction_two) + epsilon)
    updated = (
        weight_rows.astype(jnp.float32) * (1.0 - learn_rate * decay_rate) - learn_rate * step_size
    ).astype(jnp.bfloat16)
    return updated, first_next, second_next


def adam_kernel(columns, owner_ref, moments_ref, *refs):
    weight_refs, refs = refs[:columns], refs[columns:]
    part_refs, (new_ref, first_ref, second_ref, gradient, inverse_ref) = refs[:-5], refs[-5:]
    for slot in range(moments_ref.shape[0]):
        inverse_ref[owner_ref[slot]] = slot
    total = part_refs[0][0].astype(jnp.float32)
    for part_ref in part_refs[1:]:
        total = total + part_ref[0].astype(jnp.float32)
    gradient[...] = total.T
    for pair in range(moments_ref.shape[0] // 2):
        even = moments_ref[inverse_ref[2 * pair]].astype(jnp.float32)
        odd = moments_ref[inverse_ref[2 * pair + 1]].astype(jnp.float32)
        rows = pl.ds(pair * 2 * SUB, 2 * SUB)
        new_ref[rows, :], first_ref[rows, :], second_ref[rows, :] = adam(
            jnp.concatenate([ref[rows, :] for ref in weight_refs], axis=1),
            jnp.concatenate([even[:SUB], odd[:SUB]], axis=0),
            jnp.concatenate([even[SUB:], odd[SUB:]], axis=0),
            gradient[rows, :],
        )


def adam_rows(parts, moments, weight_rows, owners):
    row_block, columns = weight_rows[0].shape
    width = columns * len(weight_rows)
    whole = pl.BlockSpec((row_block, width), lambda i, *_: (0, 0))
    return pl.pallas_call(
        functools.partial(adam_kernel, len(weight_rows)),
        grid_spec=pltpu.PrefetchScalarGridSpec(
            num_scalar_prefetch=1,
            grid=(1,),
            in_specs=[pl.BlockSpec(moments.shape, lambda i, *_: (0, 0, 0))]
            + [pl.BlockSpec((row_block, columns), lambda i, *_: (0, 0))] * len(weight_rows)
            + [pl.BlockSpec((1, width, row_block), lambda i, *_: (0, 0, 0))] * len(parts),
            out_specs=[whole] * 3,
            scratch_shapes=[
                pltpu.VMEM((row_block, width), jnp.float32),
                pltpu.SMEM((moments.shape[0],), jnp.int32),
            ],
        ),
        out_shape=[
            jax.ShapeDtypeStruct((row_block, width), jnp.bfloat16),
            jax.ShapeDtypeStruct((row_block, width), jnp.float32),
            jax.ShapeDtypeStruct((row_block, width), jnp.float32),
        ],
        compiler_params=pltpu.CompilerParams(vmem_limit_bytes=12 * MIB),
        cost_estimate=cost(20 * row_block * width, 16 * row_block * width),
        name="adam_rows",
    )(owners, moments, *weight_rows, *parts)


class Grid:
    def __init__(self, groups, shards):
        self.shards = shards
        self.cores = 2 if groups % 2 == 0 else 1
        self.minor = 2 if shards % 2 == 0 else 1
        self.outer = groups // self.cores
        self.far = shards // self.minor
        self.swaps = self.cores == 2 and self.minor == self.outer
        self.near, self.side = self.minor, self.outer

    def moved(self, position, core=0, near=0, side=0, far=0):
        group, shard = position // self.shards, position % self.shards
        outer, on = group // self.cores, (group % self.cores + core) % self.cores
        depth, minor = shard // self.minor, shard % self.minor
        swapped = on if self.swaps else 0
        minor = (minor + near + (side - near) * swapped) % self.minor
        outer = (outer + side + (near - side) * swapped) % self.outer
        depth = (depth + far) % self.far
        return (outer * self.cores + on) * self.shards + depth * self.minor + minor

    def send(self, value, **steps):
        devices = self.outer * self.cores * self.shards
        pairs = [(p, self.moved(p, **steps)) for p in range(devices)]
        return lax.ppermute(value, AXES, pairs)


def rounded_sum(terms, start, count):
    total = sum(term[start : start + count].astype(jnp.float32) for term in terms)
    return total.astype(terms[0].dtype)


def sum_chunks(grid):
    half = grid.far // 2
    return [sorted({d, (grid.far - d) % grid.far}) for d in range(half + 1)]


def shard_chunks(grid):
    return sum_chunks(grid)


def tables(grid, devices):
    sums = [
        dict(core=core, near=near, side=side, far=far)
        for chunk in sum_chunks(grid)
        for core in range(grid.cores)
        for near in [*range(1, grid.near), 0]
        for side in range(grid.side)
        for far in chunk
    ]
    shards = [
        dict(core=-core, near=-near, side=-side, far=-far)
        for chunk in shard_chunks(grid)
        for core in range(grid.cores)
        for near in range(grid.near)
        for side in range(grid.side)
        for far in chunk
    ]
    return np.array(
        [[grid.moved(p, **step) for step in sums + shards] for p in range(devices)], np.int32
    )


def reduce_rows(grid, blocks_of, project_now):
    plan = []
    start = 0
    for number, chunk in enumerate(sum_chunks(grid)):
        plan.insert(0, (number, chunk, start))
        start += len(chunk)
    addends = {}
    if grid.cores > 1:
        for number, chunk, start in plan:
            block = blocks_of(1, number, start, len(chunk), None, False)[0]
            addends[number] = grid.send(block, core=1)
    held = {}
    for number, chunk, start in plan:
        parts = blocks_of(0, number, start, len(chunk), addends.get(number), True)
        held[number] = [parts[-1]]
        for step, part in enumerate(parts[:-1], 1):
            held[number].append(grid.send(part, near=step))
    projection = project_now()
    last = []
    for number, chunk, _ in plan:
        count = len(chunk)
        kept = held[number]
        ends = list(kept)
        for step in range(1, grid.side):
            part = rounded_sum(kept, step * count, count)
            ends.append(grid.send(part, side=step))
        held[number] = ends
    for number, chunk, _ in plan:
        ends = held[number]
        for index, far in enumerate(chunk):
            if not far:
                last.extend(ends)
                continue
            last.append(grid.send(rounded_sum(ends, index, 1), far=far))
    return last, projection


def gather_shards(grid, own):
    arrived = {far: grid.send(own, far=far) for far in range(1, grid.far)}
    arrived[0] = own
    pieces, marks = [], []
    for chunk in shard_chunks(grid):
        base = joined([arrived[far] for far in chunk])
        sides = [grid.send(base, side=step) for step in range(1, grid.side)]
        both = [joined([base] + sides)]
        nears = [grid.send(part, near=step) for step in range(1, grid.near) for part in both]
        marks.append((sides, nears, [arrived[far] for far in chunk]))
        pieces += both + nears
        for core in range(1, grid.cores):
            pieces += [grid.send(part, core=core) for part in both + nears]
    return pieces, marks


def joined(arrays):
    return arrays[0] if len(arrays) == 1 else jnp.concatenate(arrays, axis=0)


def body(tokens, cotangent, old_weight, old_first, old_second, old_owner, new_owner):
    devices = lax.axis_size(AXES)
    groups = lax.axis_size("rep")
    shards = lax.axis_size("fsdp")
    features = tokens.shape[1]
    row_block, width = old_weight.shape
    strip = row_block * width // devices
    grid = Grid(groups, shards)
    me = lax.axis_index(AXES)
    by_tile = row_block == devices * SUB and width % 128 == 0 and devices % 4 == 0

    row = lax.dynamic_index_in_dim(jnp.asarray(tables(grid, devices)), me, 0, keepdims=False)
    per_far = grid.near * grid.side
    own = (grid.near - 1) * grid.side * len(sum_chunks(grid)[0])

    cuts = COLUMNS if by_tile and width % (128 * COLUMNS) == 0 else 1
    gathered = [gather_shards(grid, part[None]) for part in jnp.split(old_weight, cuts, axis=1)]
    marks = [mark for _, part in gathered for mark in part]
    if by_tile:
        packed = pack_moments(old_first, old_second, new_owner, groups)
    else:
        slot_ids = jnp.arange(devices, dtype=jnp.int32)
        placing = jnp.take(new_owner, slot_ids % shards) * groups + slot_ids // shards
        both = jnp.stack([old_first, old_second]).astype(jnp.bfloat16)
        packed = jnp.take(
            jnp.transpose(both.reshape(2, devices, strip), (1, 0, 2)), placing, axis=0
        )
    arrived = lax.all_to_all(packed, AXES, split_axis=0, concat_axis=0, tiled=True)

    turned = cotangent.T

    waits = {}
    if by_tile and len(marks) == 3:
        waits = {
            (1, 2): [packed, *marks[0][0]],
            (1, 1): marks[1][2],
            (1, 0): marks[0][1],
            (0, 2): [*marks[2][2], *marks[1][0]],
        }
    done = []

    def blocks_of(core, chunk, start, count, addend, cut):
        first = (start * grid.cores + core * count) * per_far
        per_step = grid.side * count
        after = [*waits.get((core, chunk), ()), *done[-1:]]
        blocks = grad_blocks(
            tokens, turned, row, new_owner, first, grid.near, per_step, addend, cut, after
        )
        done.append(blocks[0])
        return blocks

    def project_now():
        if not by_tile:
            return ()
        projected, weight_rows = None, []
        for part, (pieces, _) in enumerate(gathered):
            projected, rows = project(
                tokens, pieces, row, devices, own, old_owner, new_owner, part, cuts, projected
            )
            weight_rows.append(rows)
        return projected, weight_rows

    parts, projection = reduce_rows(grid, blocks_of, project_now)
    if by_tile:
        projected, weight_rows = projection
        return (projected, *adam_rows(parts, arrived, weight_rows, old_owner))
    inverse = jnp.zeros((devices,), jnp.int32).at[old_owner].set(slot_ids)
    held = jnp.zeros((devices, devices, strip), jnp.bfloat16)
    held = held.at[jnp.take(old_owner, row[devices:])].set(
        joined(gathered[0][0]).reshape(devices, devices, strip)
    )
    logical = jnp.transpose(held, (1, 0, 2)).reshape(features, width)
    projected = jnp.dot(tokens, logical, preferred_element_type=jnp.float32).astype(jnp.bfloat16)
    own_block = jnp.take(placing, me)
    weight_rows = lax.dynamic_slice_in_dim(logical, own_block * row_block, row_block, 0)
    moved = jnp.transpose(jnp.take(arrived, inverse, axis=0), (1, 0, 2))
    first_rows, second_rows = moved.astype(jnp.float32).reshape(2, row_block, width)
    gradient = sum(part[0].astype(jnp.float32) for part in parts).T
    return (projected, *adam(weight_rows, first_rows, second_rows, gradient))


def solution(mesh):
    placed = P(AXES, None)
    return jax.shard_map(
        body,
        mesh=mesh,
        in_specs=(placed,) * 5 + (P(), P()),
        out_specs=(placed,) * 4,
        check_vma=False,
    )
```

```python
import functools
import jax
import jax.numpy as jnp
import numpy as np
from jax import lax
from jax.experimental import pallas as pl
from jax.experimental.pallas import tpu as pltpu
from jax.sharding import PartitionSpec as P

beta_one = 0.9
beta_two = 0.95
learn_rate = 0.001
decay_rate = 0.1
epsilon = 1e-08
correction_one = 1.0 - 0.9**10
correction_two = 1.0 - 0.95**10

AXES = ("rep", "fsdp")
GRANT = 48 * 1024 * 1024
SUB = 8


def cost(flops, moved):
    return pl.CostEstimate(flops=flops, bytes_accessed=moved, transcendentals=0)


def block_at(new_ref, groups, position):
    shards = new_ref.shape[0]
    return new_ref[lax.rem(position, shards)] * groups + lax.div(position, shards)


def grad_kernel(per_step, adds, row_ref, new_ref, *refs):
    token_refs, turned_ref, refs = refs[:per_step], refs[per_step], refs[per_step + 1 :]
    out_refs = refs[adds:]

    def write(out_ref):
        wide = jnp.concatenate([token_ref[...] for token_ref in token_refs], axis=1)
        blocks = jnp.dot(turned_ref[...], wide, preferred_element_type=jnp.float32)
        row_block = out_ref.shape[2]
        for slot in range(per_step):
            block = blocks[:, slot * row_block : (slot + 1) * row_block]
            if adds:
                block = block + refs[0][slot].astype(jnp.float32)
            out_ref[slot] = block.astype(out_ref.dtype)

    if len(out_refs) == 1:
        write(out_refs[0])
        return
    for step, out_ref in enumerate(out_refs):
        pl.when(pl.program_id(0) == step)(functools.partial(write, out_ref))


def grad_blocks(tokens, turned, row, new_owner, first, steps, per_step, addend=None, cut=False):
    rows, features = tokens.shape
    width = turned.shape[0]
    blocks = steps * per_step
    groups = lax.axis_size("rep")
    row_block = features // (groups * new_owner.shape[0])
    if row_block % 128:
        chosen = row[first : first + blocks]
        chosen = jnp.take(new_owner, chosen % new_owner.shape[0]) * groups + (
            chosen // new_owner.shape[0]
        )
        whole = jnp.dot(turned, tokens, preferred_element_type=jnp.float32)
        parts = jnp.transpose(whole.reshape(width, features // row_block, row_block), (1, 0, 2))
        parts = jnp.take(parts, chosen, axis=0)
        if addend is not None:
            parts = parts + addend.astype(jnp.float32)
        parts = parts.astype(jnp.bfloat16)
        return list(jnp.split(parts, steps)) if cut else [parts]

    def token_map(slot):
        return lambda i, row_ref, new_ref: (
            0,
            block_at(new_ref, groups, row_ref[first + i * per_step + slot]),
        )

    block = pl.BlockSpec((per_step, width, row_block), lambda i, *_: (i, 0, 0))
    fixed = pl.BlockSpec((per_step, width, row_block), lambda i, *_: (0, 0, 0))
    added = [] if addend is None else [addend]
    outs = steps if cut else 1
    return pl.pallas_call(
        functools.partial(grad_kernel, per_step, len(added)),
        grid_spec=pltpu.PrefetchScalarGridSpec(
            num_scalar_prefetch=2,
            grid=(steps,),
            in_specs=[pl.BlockSpec((rows, row_block), token_map(s)) for s in range(per_step)]
            + [pl.BlockSpec((width, rows), lambda i, *_: (0, 0))]
            + [block] * len(added),
            out_specs=[fixed if cut else block] * outs,
        ),
        out_shape=[jax.ShapeDtypeStruct((blocks // outs, width, row_block), jnp.bfloat16)] * outs,
        compiler_params=pltpu.CompilerParams(vmem_limit_bytes=GRANT),
        cost_estimate=cost(
            2 * rows * width * blocks * row_block,
            2 * blocks * row_block * (rows + width * (1 + len(added))) + 2 * rows * width,
        ),
        name="weight_gradient",
    )(row, new_owner, *([tokens] * per_step), turned, *added)


def pack_kernel(groups, new_ref, first_ref, second_ref, out_ref):
    for slot in range(out_ref.shape[0]):
        block = block_at(new_ref, groups, slot)
        rows = pl.ds(pl.multiple_of(block * SUB, SUB), SUB)
        pair = jnp.concatenate([first_ref[rows, :], second_ref[rows, :]], axis=0)
        out_ref[slot] = pair.astype(out_ref.dtype)


def pack_moments(first, second, new_owner, groups):
    devices = new_owner.shape[0] * groups
    width = first.shape[1]
    return pl.pallas_call(
        functools.partial(pack_kernel, groups),
        in_specs=[
            pl.BlockSpec(memory_space=pltpu.SMEM),
            pl.BlockSpec(memory_space=pltpu.VMEM),
            pl.BlockSpec(memory_space=pltpu.VMEM),
        ],
        out_specs=pl.BlockSpec(memory_space=pltpu.VMEM),
        out_shape=jax.ShapeDtypeStruct((devices, 2 * SUB, width), jnp.bfloat16),
        cost_estimate=cost(0, 12 * first.size),
        name="pack_moments",
    )(new_owner, first, second)


def project_kernel(groups, first, own, row_ref, old_ref, new_ref, token_ref, *refs):
    piece_refs, (out_ref, rows_ref, held, logical, sems) = refs[:-5], refs[-5:]
    devices, row_block, _ = held.shape

    @pl.when(pl.program_id(0) == 0)
    def _():
        copies = []
        for piece_ref in piece_refs:
            for index in range(piece_ref.shape[0]):
                slot = len(copies)
                target = held.at[old_ref[row_ref[first + slot]]]
                copies.append(pltpu.make_async_copy(piece_ref.at[index], target, sems.at[slot]))
        for copy in copies:
            copy.start()
        for copy in copies:
            copy.wait()

        def place(pair, carry):
            for block in range(0, devices, 2):
                span = pl.ds(block * SUB, 2 * SUB)
                top = held[2 * pair, span, :]
                low = held[2 * pair + 1, span, :]
                for half in range(2):
                    part = slice(half * SUB, (half + 1) * SUB)
                    start = (block + half) * row_block + pair * 2 * SUB
                    logical[pl.ds(pl.multiple_of(start, 2 * SUB), 2 * SUB), :] = jnp.concatenate(
                        [top[part], low[part]], axis=0
                    )
            return carry

        lax.fori_loop(0, devices // 2, place, 0)
        start = block_at(new_ref, groups, row_ref[own]) * row_block
        start = pl.multiple_of(start, row_block)
        rows_ref[...] = logical[pl.ds(start, row_block), :]

    out_ref[...] = jnp.dot(
        token_ref[...], logical[...], preferred_element_type=jnp.float32
    ).astype(out_ref.dtype)


def project(tokens, pieces, row, first, own, old_owner, new_owner):
    rows, features = tokens.shape
    _, row_block, width = pieces[0].shape
    devices = old_owner.shape[0]
    tile = rows // 4
    return pl.pallas_call(
        functools.partial(project_kernel, devices // new_owner.shape[0], first, own),
        grid_spec=pltpu.PrefetchScalarGridSpec(
            num_scalar_prefetch=3,
            grid=(rows // tile,),
            in_specs=[pl.BlockSpec((tile, features), lambda i, *_: (i, 0))]
            + [pl.BlockSpec(memory_space=pl.ANY)] * len(pieces),
            out_specs=[
                pl.BlockSpec((tile, width), lambda i, *_: (i, 0)),
                pl.BlockSpec((row_block, width), lambda i, *_: (0, 0)),
            ],
            scratch_shapes=[
                pltpu.VMEM((devices, row_block, width), jnp.bfloat16),
                pltpu.VMEM((features, width), jnp.bfloat16),
                pltpu.SemaphoreType.DMA((devices,)),
            ],
        ),
        out_shape=[
            jax.ShapeDtypeStruct((rows, width), jnp.bfloat16),
            jax.ShapeDtypeStruct((row_block, width), jnp.bfloat16),
        ],
        compiler_params=pltpu.CompilerParams(vmem_limit_bytes=GRANT),
        cost_estimate=cost(
            2 * rows * width * features, 2 * (rows * features + features * width + rows * width)
        ),
        name="project",
    )(row, old_owner, new_owner, tokens, *pieces)


def adam(weight_rows, first_rows, second_rows, gradient):
    first_next = beta_one * first_rows + (1.0 - beta_one) * gradient
    second_next = beta_two * second_rows + (1.0 - beta_two) * gradient * gradient
    step_size = first_next / correction_one / (jnp.sqrt(second_next / correction_two) + epsilon)
    updated = (
        weight_rows.astype(jnp.float32) * (1.0 - learn_rate * decay_rate) - learn_rate * step_size
    ).astype(jnp.bfloat16)
    return updated, first_next, second_next


def adam_kernel(owner_ref, moments_ref, weight_ref, *refs):
    part_refs, (new_ref, first_ref, second_ref, gradient, inverse_ref) = refs[:-5], refs[-5:]
    for slot in range(moments_ref.shape[0]):
        inverse_ref[owner_ref[slot]] = slot
    total = part_refs[0][0].astype(jnp.float32)
    for part_ref in part_refs[1:]:
        total = total + part_ref[0].astype(jnp.float32)
    gradient[...] = total.T
    for pair in range(moments_ref.shape[0] // 2):
        even = moments_ref[inverse_ref[2 * pair]].astype(jnp.float32)
        odd = moments_ref[inverse_ref[2 * pair + 1]].astype(jnp.float32)
        rows = pl.ds(pair * 2 * SUB, 2 * SUB)
        new_ref[rows, :], first_ref[rows, :], second_ref[rows, :] = adam(
            weight_ref[rows, :],
            jnp.concatenate([even[:SUB], odd[:SUB]], axis=0),
            jnp.concatenate([even[SUB:], odd[SUB:]], axis=0),
            gradient[rows, :],
        )


def adam_rows(parts, moments, weight_rows, owners):
    row_block, width = weight_rows.shape
    whole = pl.BlockSpec((row_block, width), lambda i, *_: (0, 0))
    return pl.pallas_call(
        adam_kernel,
        grid_spec=pltpu.PrefetchScalarGridSpec(
            num_scalar_prefetch=1,
            grid=(1,),
            in_specs=[pl.BlockSpec(moments.shape, lambda i, *_: (0, 0, 0)), whole]
            + [pl.BlockSpec((1, width, row_block), lambda i, *_: (0, 0, 0))] * len(parts),
            out_specs=[whole] * 3,
            scratch_shapes=[
                pltpu.VMEM((row_block, width), jnp.float32),
                pltpu.SMEM((moments.shape[0],), jnp.int32),
            ],
        ),
        out_shape=[
            jax.ShapeDtypeStruct((row_block, width), jnp.bfloat16),
            jax.ShapeDtypeStruct((row_block, width), jnp.float32),
            jax.ShapeDtypeStruct((row_block, width), jnp.float32),
        ],
        compiler_params=pltpu.CompilerParams(vmem_limit_bytes=GRANT),
        cost_estimate=cost(20 * row_block * width, 16 * row_block * width),
        name="adam_rows",
    )(owners, moments, weight_rows, *parts)


class Grid:
    def __init__(self, groups, shards):
        self.shards = shards
        self.cores = 2 if groups % 2 == 0 else 1
        self.minor = 2 if shards % 2 == 0 else 1
        self.outer = groups // self.cores
        self.far = shards // self.minor
        self.swaps = self.cores == 2 and self.minor == self.outer
        self.near, self.side = self.minor, self.outer

    def moved(self, position, core=0, near=0, side=0, far=0):
        group, shard = position // self.shards, position % self.shards
        outer, on = group // self.cores, (group % self.cores + core) % self.cores
        depth, minor = shard // self.minor, shard % self.minor
        swapped = on if self.swaps else 0
        minor = (minor + near + (side - near) * swapped) % self.minor
        outer = (outer + side + (near - side) * swapped) % self.outer
        depth = (depth + far) % self.far
        return (outer * self.cores + on) * self.shards + depth * self.minor + minor

    def send(self, value, **steps):
        devices = self.outer * self.cores * self.shards
        pairs = [(p, self.moved(p, **steps)) for p in range(devices)]
        return lax.ppermute(value, AXES, pairs)


def rounded_sum(*terms):
    total = terms[0].astype(jnp.float32)
    for term in terms[1:]:
        total = total + term.astype(jnp.float32)
    return total.astype(terms[0].dtype)


def chunks(grid):
    half = grid.far // 2
    return [sorted({d, (grid.far - d) % grid.far}) for d in range(half + 1)]


def tables(grid, devices):
    sums = [
        dict(core=core, near=near, side=side, far=far)
        for chunk in chunks(grid)
        for core in range(grid.cores)
        for near in [*range(1, grid.near), 0]
        for side in range(grid.side)
        for far in chunk
    ]
    shards = [
        dict(core=-core, near=-near, side=-side, far=-far)
        for chunk in chunks(grid)
        for core in range(grid.cores)
        for near in range(grid.near)
        for side in range(grid.side)
        for far in chunk
    ]
    return np.array(
        [[grid.moved(p, **step) for step in sums + shards] for p in range(devices)], np.int32
    )


def reduce_rows(grid, blocks_of):
    last = []
    start = grid.far
    for chunk in reversed(chunks(grid)):
        count = len(chunk)
        start -= count
        addend = None
        if grid.cores > 1:
            addend = grid.send(blocks_of(1, start, count, None, False)[0], core=1)
        parts = blocks_of(0, start, count, addend, True)
        kept = [parts[-1]]
        for step, part in enumerate(parts[:-1], 1):
            kept.append(grid.send(part, near=step))
        ends = list(kept)
        for step in range(1, grid.side):
            cut = slice(step * count, (step + 1) * count)
            ends.append(grid.send(rounded_sum(*[t[cut] for t in kept]), side=step))
        if chunk == [0]:
            last.extend(ends)
            continue
        for index, far in enumerate(chunk):
            cut = slice(index, index + 1)
            last.append(grid.send(rounded_sum(*[t[cut] for t in ends]), far=far))
    return last


def gather_shards(grid, own):
    arrived = {far: grid.send(own, far=far) for far in range(1, grid.far)}
    arrived[0] = own
    pieces = []
    for chunk in chunks(grid):
        base = joined([arrived[far] for far in chunk])
        plane = joined([base] + [grid.send(base, side=step) for step in range(1, grid.side)])
        both = [plane] + [grid.send(plane, near=step) for step in range(1, grid.near)]
        pieces += both
        for core in range(1, grid.cores):
            pieces += [grid.send(part, core=core) for part in both]
    return pieces


def joined(arrays):
    return arrays[0] if len(arrays) == 1 else jnp.concatenate(arrays, axis=0)


def body(tokens, cotangent, old_weight, old_first, old_second, old_owner, new_owner):
    devices = lax.axis_size(AXES)
    groups = lax.axis_size("rep")
    shards = lax.axis_size("fsdp")
    features = tokens.shape[1]
    row_block, width = old_weight.shape
    strip = row_block * width // devices
    grid = Grid(groups, shards)
    me = lax.axis_index(AXES)
    by_tile = row_block == devices * SUB and width % 128 == 0 and devices % 2 == 0

    row = lax.dynamic_index_in_dim(jnp.asarray(tables(grid, devices)), me, 0, keepdims=False)
    per_far = grid.near * grid.side
    own = (grid.near - 1) * grid.side

    pieces = gather_shards(grid, old_weight[None])
    if by_tile:
        packed = pack_moments(old_first, old_second, new_owner, groups)
    else:
        slot_ids = jnp.arange(devices, dtype=jnp.int32)
        placing = jnp.take(new_owner, slot_ids % shards) * groups + slot_ids // shards
        both = jnp.stack([old_first, old_second]).astype(jnp.bfloat16)
        packed = jnp.take(
            jnp.transpose(both.reshape(2, devices, strip), (1, 0, 2)), placing, axis=0
        )
    arrived = lax.all_to_all(packed, AXES, split_axis=0, concat_axis=0, tiled=True)

    turned = cotangent.T

    def blocks_of(core, start, count, addend, cut):
        first = (start * grid.cores + core * count) * per_far
        per_step = grid.side * count
        return grad_blocks(
            tokens, turned, row, new_owner, first, grid.near, per_step, addend, cut
        )

    parts = reduce_rows(grid, blocks_of)
    if by_tile:
        projected, weight_rows = project(tokens, pieces, row, devices, own, old_owner, new_owner)
        return (projected, *adam_rows(parts, arrived, weight_rows, old_owner))
    inverse = jnp.zeros((devices,), jnp.int32).at[old_owner].set(slot_ids)
    held = jnp.zeros((devices, devices, strip), jnp.bfloat16)
    held = held.at[jnp.take(old_owner, row[devices:])].set(
        joined(pieces).reshape(devices, devices, strip)
    )
    logical = jnp.transpose(held, (1, 0, 2)).reshape(features, width)
    projected = jnp.dot(tokens, logical, preferred_element_type=jnp.float32).astype(jnp.bfloat16)
    own_block = jnp.take(placing, me)
    weight_rows = lax.dynamic_slice_in_dim(logical, own_block * row_block, row_block, 0)
    moved = jnp.transpose(jnp.take(arrived, inverse, axis=0), (1, 0, 2))
    first_rows, second_rows = moved.astype(jnp.float32).reshape(2, row_block, width)
    gradient = sum(part[0].astype(jnp.float32) for part in parts).T
    return (projected, *adam(weight_rows, first_rows, second_rows, gradient))


def solution(mesh):
    placed = P(AXES, None)
    return jax.shard_map(
        body,
        mesh=mesh,
        in_specs=(placed,) * 5 + (P(), P()),
        out_specs=(placed,) * 4,
        check_vma=False,
    )
```

```python
import functools
import jax
import jax.numpy as jnp
import numpy as np
from jax import lax
from jax.experimental import pallas as pl
from jax.experimental.pallas import tpu as pltpu
from jax.sharding import PartitionSpec as P

beta_one = 0.9
beta_two = 0.95
learn_rate = 0.001
decay_rate = 0.1
epsilon = 1e-08
correction_one = 1.0 - 0.9**10
correction_two = 1.0 - 0.95**10

AXES = ("rep", "fsdp")
GRANT = 45 * 1024 * 1024
SUB = 8


def cost(flops, moved):
    return pl.CostEstimate(flops=flops, bytes_accessed=moved, transcendentals=0)


def block_at(new_ref, groups, position):
    shards = new_ref.shape[0]
    return new_ref[lax.rem(position, shards)] * groups + lax.div(position, shards)


def grad_kernel(per_step, adds, outs, row_ref, new_ref, *refs):
    token_refs, turned_ref, refs = refs[:per_step], refs[per_step], refs[per_step + 1 :]
    out_refs = refs[-outs:]

    def write(out_ref):
        for slot, token_ref in enumerate(token_refs):
            block = jnp.dot(turned_ref[...], token_ref[...], preferred_element_type=jnp.float32)
            if adds:
                block = block + refs[0][slot].astype(jnp.float32)
            out_ref[slot] = block.astype(out_ref.dtype)

    if len(out_refs) == 1:
        write(out_refs[0])
        return
    for step, out_ref in enumerate(out_refs):
        pl.when(pl.program_id(0) == step)(functools.partial(write, out_ref))


def grad_blocks(
    tokens, turned, row, new_owner, first, steps, per_step, addend=None, cut=False, after=()
):
    rows, features = tokens.shape
    width = turned.shape[0]
    blocks = steps * per_step
    groups = lax.axis_size("rep")
    row_block = features // (groups * new_owner.shape[0])
    if row_block % 128:
        chosen = row[first : first + blocks]
        chosen = jnp.take(new_owner, chosen % new_owner.shape[0]) * groups + (
            chosen // new_owner.shape[0]
        )
        whole = jnp.dot(turned, tokens, preferred_element_type=jnp.float32)
        parts = jnp.transpose(whole.reshape(width, features // row_block, row_block), (1, 0, 2))
        parts = jnp.take(parts, chosen, axis=0)
        if addend is not None:
            parts = parts + addend.astype(jnp.float32)
        parts = parts.astype(jnp.bfloat16)
        return list(jnp.split(parts, steps)) if cut else [parts]

    def token_map(slot):
        return lambda i, row_ref, new_ref: (
            0,
            block_at(new_ref, groups, row_ref[first + i * per_step + slot]),
        )

    block = pl.BlockSpec((per_step, width, row_block), lambda i, *_: (i, 0, 0))
    fixed = pl.BlockSpec((per_step, width, row_block), lambda i, *_: (0, 0, 0))
    added = [] if addend is None else [addend]
    outs = steps if cut else 1
    return pl.pallas_call(
        functools.partial(grad_kernel, per_step, len(added), outs),
        grid_spec=pltpu.PrefetchScalarGridSpec(
            num_scalar_prefetch=2,
            grid=(steps,),
            in_specs=[pl.BlockSpec((rows, row_block), token_map(s)) for s in range(per_step)]
            + [pl.BlockSpec((width, rows), lambda i, *_: (0, 0))]
            + [block] * len(added)
            + [pl.BlockSpec(memory_space=pl.ANY)] * len(after),
            out_specs=[fixed if cut else block] * outs,
        ),
        out_shape=[jax.ShapeDtypeStruct((blocks // outs, width, row_block), jnp.bfloat16)] * outs,
        compiler_params=pltpu.CompilerParams(vmem_limit_bytes=GRANT),
        cost_estimate=cost(
            2 * rows * width * blocks * row_block,
            2 * blocks * row_block * (rows + width * (1 + len(added))) + 2 * rows * width,
        ),
        name="weight_gradient",
    )(row, new_owner, *([tokens] * per_step), turned, *added, *after)


def pack_kernel(groups, new_ref, first_ref, second_ref, out_ref):
    for slot in range(out_ref.shape[0]):
        block = block_at(new_ref, groups, slot)
        rows = pl.ds(pl.multiple_of(block * SUB, SUB), SUB)
        pair = jnp.concatenate([first_ref[rows, :], second_ref[rows, :]], axis=0)
        out_ref[slot] = pair.astype(out_ref.dtype)


def pack_moments(first, second, new_owner, groups):
    devices = new_owner.shape[0] * groups
    width = first.shape[1]
    return pl.pallas_call(
        functools.partial(pack_kernel, groups),
        in_specs=[
            pl.BlockSpec(memory_space=pltpu.SMEM),
            pl.BlockSpec(memory_space=pltpu.VMEM),
            pl.BlockSpec(memory_space=pltpu.VMEM),
        ],
        out_specs=pl.BlockSpec(memory_space=pltpu.VMEM),
        out_shape=jax.ShapeDtypeStruct((devices, 2 * SUB, width), jnp.bfloat16),
        cost_estimate=cost(0, 12 * first.size),
        name="pack_moments",
    )(new_owner, first, second)


def project_kernel(groups, first, own, row_ref, old_ref, new_ref, token_ref, *refs):
    piece_refs, (out_ref, rows_ref, held, logical, sems) = refs[:-5], refs[-5:]
    devices, row_block, _ = held.shape

    @pl.when(pl.program_id(0) == 0)
    def _():
        copies = []
        for piece_ref in piece_refs:
            for index in range(piece_ref.shape[0]):
                slot = len(copies)
                target = held.at[old_ref[row_ref[first + slot]]]
                copies.append(pltpu.make_async_copy(piece_ref.at[index], target, sems.at[slot]))
        for copy in copies:
            copy.start()
        for copy in copies:
            copy.wait()

        def place(pair, carry):
            for block in range(0, devices, 2):
                span = pl.ds(block * SUB, 2 * SUB)
                top = held[2 * pair, span, :]
                low = held[2 * pair + 1, span, :]
                for half in range(2):
                    part = slice(half * SUB, (half + 1) * SUB)
                    start = (block + half) * row_block + pair * 2 * SUB
                    logical[pl.ds(pl.multiple_of(start, 2 * SUB), 2 * SUB), :] = jnp.concatenate(
                        [top[part], low[part]], axis=0
                    )
            return carry

        lax.fori_loop(0, devices // 2, place, 0)
        start = block_at(new_ref, groups, row_ref[own]) * row_block
        start = pl.multiple_of(start, row_block)
        rows_ref[...] = logical[pl.ds(start, row_block), :]

    out_ref[...] = jnp.dot(
        token_ref[...], logical[...], preferred_element_type=jnp.float32
    ).astype(out_ref.dtype)


def project(tokens, pieces, row, first, own, old_owner, new_owner):
    rows, features = tokens.shape
    _, row_block, width = pieces[0].shape
    devices = old_owner.shape[0]
    tile = rows // 4
    return pl.pallas_call(
        functools.partial(project_kernel, devices // new_owner.shape[0], first, own),
        grid_spec=pltpu.PrefetchScalarGridSpec(
            num_scalar_prefetch=3,
            grid=(rows // tile,),
            in_specs=[pl.BlockSpec((tile, features), lambda i, *_: (i, 0))]
            + [pl.BlockSpec(memory_space=pl.ANY)] * len(pieces),
            out_specs=[
                pl.BlockSpec((tile, width), lambda i, *_: (i, 0)),
                pl.BlockSpec((row_block, width), lambda i, *_: (0, 0)),
            ],
            scratch_shapes=[
                pltpu.VMEM((devices, row_block, width), jnp.bfloat16),
                pltpu.VMEM((features, width), jnp.bfloat16),
                pltpu.SemaphoreType.DMA((devices,)),
            ],
        ),
        out_shape=[
            jax.ShapeDtypeStruct((rows, width), jnp.bfloat16),
            jax.ShapeDtypeStruct((row_block, width), jnp.bfloat16),
        ],
        compiler_params=pltpu.CompilerParams(vmem_limit_bytes=GRANT),
        cost_estimate=cost(
            2 * rows * width * features, 2 * (rows * features + features * width + rows * width)
        ),
        name="project",
    )(row, old_owner, new_owner, tokens, *pieces)


def adam(weight_rows, first_rows, second_rows, gradient):
    first_next = beta_one * first_rows + (1.0 - beta_one) * gradient
    second_next = beta_two * second_rows + (1.0 - beta_two) * gradient * gradient
    step_size = first_next / correction_one / (jnp.sqrt(second_next / correction_two) + epsilon)
    updated = (
        weight_rows.astype(jnp.float32) * (1.0 - learn_rate * decay_rate) - learn_rate * step_size
    ).astype(jnp.bfloat16)
    return updated, first_next, second_next


def adam_kernel(owner_ref, moments_ref, weight_ref, *refs):
    part_refs, (new_ref, first_ref, second_ref, gradient, inverse_ref) = refs[:-5], refs[-5:]
    for slot in range(moments_ref.shape[0]):
        inverse_ref[owner_ref[slot]] = slot
    total = part_refs[0][0].astype(jnp.float32)
    for part_ref in part_refs[1:]:
        total = total + part_ref[0].astype(jnp.float32)
    gradient[...] = total.T
    for pair in range(moments_ref.shape[0] // 2):
        even = moments_ref[inverse_ref[2 * pair]].astype(jnp.float32)
        odd = moments_ref[inverse_ref[2 * pair + 1]].astype(jnp.float32)
        rows = pl.ds(pair * 2 * SUB, 2 * SUB)
        new_ref[rows, :], first_ref[rows, :], second_ref[rows, :] = adam(
            weight_ref[rows, :],
            jnp.concatenate([even[:SUB], odd[:SUB]], axis=0),
            jnp.concatenate([even[SUB:], odd[SUB:]], axis=0),
            gradient[rows, :],
        )


def adam_rows(parts, moments, weight_rows, owners):
    row_block, width = weight_rows.shape
    whole = pl.BlockSpec((row_block, width), lambda i, *_: (0, 0))
    return pl.pallas_call(
        adam_kernel,
        grid_spec=pltpu.PrefetchScalarGridSpec(
            num_scalar_prefetch=1,
            grid=(1,),
            in_specs=[pl.BlockSpec(moments.shape, lambda i, *_: (0, 0, 0)), whole]
            + [pl.BlockSpec((1, width, row_block), lambda i, *_: (0, 0, 0))] * len(parts),
            out_specs=[whole] * 3,
            scratch_shapes=[
                pltpu.VMEM((row_block, width), jnp.float32),
                pltpu.SMEM((moments.shape[0],), jnp.int32),
            ],
        ),
        out_shape=[
            jax.ShapeDtypeStruct((row_block, width), jnp.bfloat16),
            jax.ShapeDtypeStruct((row_block, width), jnp.float32),
            jax.ShapeDtypeStruct((row_block, width), jnp.float32),
        ],
        compiler_params=pltpu.CompilerParams(vmem_limit_bytes=GRANT),
        cost_estimate=cost(20 * row_block * width, 16 * row_block * width),
        name="adam_rows",
    )(owners, moments, weight_rows, *parts)


class Grid:
    def __init__(self, groups, shards):
        self.shards = shards
        self.cores = 2 if groups % 2 == 0 else 1
        self.minor = 2 if shards % 2 == 0 else 1
        self.outer = groups // self.cores
        self.far = shards // self.minor
        self.swaps = self.cores == 2 and self.minor == self.outer
        self.near, self.side = self.minor, self.outer

    def moved(self, position, core=0, near=0, side=0, far=0):
        group, shard = position // self.shards, position % self.shards
        outer, on = group // self.cores, (group % self.cores + core) % self.cores
        depth, minor = shard // self.minor, shard % self.minor
        swapped = on if self.swaps else 0
        minor = (minor + near + (side - near) * swapped) % self.minor
        outer = (outer + side + (near - side) * swapped) % self.outer
        depth = (depth + far) % self.far
        return (outer * self.cores + on) * self.shards + depth * self.minor + minor

    def send(self, value, **steps):
        devices = self.outer * self.cores * self.shards
        pairs = [(p, self.moved(p, **steps)) for p in range(devices)]
        return lax.ppermute(value, AXES, pairs)


def rounded_sum(*terms):
    total = terms[0].astype(jnp.float32)
    for term in terms[1:]:
        total = total + term.astype(jnp.float32)
    return total.astype(terms[0].dtype)


def chunks(grid):
    half = grid.far // 2
    return [sorted({d, (grid.far - d) % grid.far}) for d in range(half + 1)]


def tables(grid, devices):
    sums = [
        dict(core=core, near=near, side=side, far=far)
        for chunk in chunks(grid)
        for core in range(grid.cores)
        for near in [*range(1, grid.near), 0]
        for side in range(grid.side)
        for far in chunk
    ]
    shards = [
        dict(core=-core, near=-near, side=-side, far=-far)
        for chunk in chunks(grid)
        for core in range(grid.cores)
        for near in range(grid.near)
        for side in range(grid.side)
        for far in chunk
    ]
    return np.array(
        [[grid.moved(p, **step) for step in sums + shards] for p in range(devices)], np.int32
    )


def reduce_rows(grid, blocks_of):
    last = []
    start = grid.far
    for number, chunk in reversed(list(enumerate(chunks(grid)))):
        count = len(chunk)
        start -= count
        addend = None
        if grid.cores > 1:
            addend = grid.send(blocks_of(1, number, start, count, None, False)[0], core=1)
        parts = blocks_of(0, number, start, count, addend, True)
        kept = [parts[-1]]
        for step, part in enumerate(parts[:-1], 1):
            kept.append(grid.send(part, near=step))
        ends = list(kept)
        for step in range(1, grid.side):
            cut = slice(step * count, (step + 1) * count)
            ends.append(grid.send(rounded_sum(*[t[cut] for t in kept]), side=step))
        if chunk == [0]:
            last.extend(ends)
            continue
        for index, far in enumerate(chunk):
            cut = slice(index, index + 1)
            last.append(grid.send(rounded_sum(*[t[cut] for t in ends]), far=far))
    return last


def gather_shards(grid, own):
    arrived = {far: grid.send(own, far=far) for far in range(1, grid.far)}
    arrived[0] = own
    pieces, marks = [], []
    for chunk in chunks(grid):
        base = joined([arrived[far] for far in chunk])
        sides = [grid.send(base, side=step) for step in range(1, grid.side)]
        plane = joined([base] + sides)
        both = [plane] + [grid.send(plane, near=step) for step in range(1, grid.near)]
        marks.append((sides, both[1:], [arrived[far] for far in chunk]))
        pieces += both
        for core in range(1, grid.cores):
            pieces += [grid.send(part, core=core) for part in both]
    return pieces, marks


def joined(arrays):
    return arrays[0] if len(arrays) == 1 else jnp.concatenate(arrays, axis=0)


def body(tokens, cotangent, old_weight, old_first, old_second, old_owner, new_owner):
    devices = lax.axis_size(AXES)
    groups = lax.axis_size("rep")
    shards = lax.axis_size("fsdp")
    features = tokens.shape[1]
    row_block, width = old_weight.shape
    strip = row_block * width // devices
    grid = Grid(groups, shards)
    me = lax.axis_index(AXES)
    by_tile = row_block == devices * SUB and width % 128 == 0 and devices % 2 == 0

    row = lax.dynamic_index_in_dim(jnp.asarray(tables(grid, devices)), me, 0, keepdims=False)
    per_far = grid.near * grid.side
    own = (grid.near - 1) * grid.side

    pieces, marks = gather_shards(grid, old_weight[None])
    if by_tile:
        packed = pack_moments(old_first, old_second, new_owner, groups)
    else:
        slot_ids = jnp.arange(devices, dtype=jnp.int32)
        placing = jnp.take(new_owner, slot_ids % shards) * groups + slot_ids // shards
        both = jnp.stack([old_first, old_second]).astype(jnp.bfloat16)
        packed = jnp.take(
            jnp.transpose(both.reshape(2, devices, strip), (1, 0, 2)), placing, axis=0
        )
    arrived = lax.all_to_all(packed, AXES, split_axis=0, concat_axis=0, tiled=True)

    turned = cotangent.T

    waits = {(0, 1): [arrived]} if by_tile else {}

    def blocks_of(core, chunk, start, count, addend, cut):
        first = (start * grid.cores + core * count) * per_far
        per_step = grid.side * count
        after = waits.get((core, chunk), ())
        return grad_blocks(
            tokens, turned, row, new_owner, first, grid.near, per_step, addend, cut, after
        )

    parts = reduce_rows(grid, blocks_of)
    if by_tile:
        projected, weight_rows = project(tokens, pieces, row, devices, own, old_owner, new_owner)
        return (projected, *adam_rows(parts, arrived, weight_rows, old_owner))
    inverse = jnp.zeros((devices,), jnp.int32).at[old_owner].set(slot_ids)
    held = jnp.zeros((devices, devices, strip), jnp.bfloat16)
    held = held.at[jnp.take(old_owner, row[devices:])].set(
        joined(pieces).reshape(devices, devices, strip)
    )
    logical = jnp.transpose(held, (1, 0, 2)).reshape(features, width)
    projected = jnp.dot(tokens, logical, preferred_element_type=jnp.float32).astype(jnp.bfloat16)
    own_block = jnp.take(placing, me)
    weight_rows = lax.dynamic_slice_in_dim(logical, own_block * row_block, row_block, 0)
    moved = jnp.transpose(jnp.take(arrived, inverse, axis=0), (1, 0, 2))
    first_rows, second_rows = moved.astype(jnp.float32).reshape(2, row_block, width)
    gradient = sum(part[0].astype(jnp.float32) for part in parts).T
    return (projected, *adam(weight_rows, first_rows, second_rows, gradient))


def solution(mesh):
    placed = P(AXES, None)
    return jax.shard_map(
        body,
        mesh=mesh,
        in_specs=(placed,) * 5 + (P(), P()),
        out_specs=(placed,) * 4,
        check_vma=False,
    )
```

```python
import functools
import jax
import jax.numpy as jnp
import numpy as np
from jax import lax
from jax.experimental import pallas as pl
from jax.experimental.pallas import tpu as pltpu
from jax.sharding import PartitionSpec as P

beta_one = 0.9
beta_two = 0.95
learn_rate = 0.001
decay_rate = 0.1
epsilon = 1e-08
correction_one = 1.0 - 0.9**10
correction_two = 1.0 - 0.95**10

AXES = ("rep", "fsdp")
GRANT = 45 * 1024 * 1024
SUB = 8


def cost(flops, moved):
    return pl.CostEstimate(flops=flops, bytes_accessed=moved, transcendentals=0)


def block_at(new_ref, groups, position):
    shards = new_ref.shape[0]
    return new_ref[lax.rem(position, shards)] * groups + lax.div(position, shards)


def grad_kernel(per_step, adds, row_ref, new_ref, *refs):
    token_refs, turned_ref, refs = refs[:per_step], refs[per_step], refs[per_step + 1 :]
    out_refs = refs[adds:]

    def write(out_ref):
        for slot, token_ref in enumerate(token_refs):
            block = jnp.dot(turned_ref[...], token_ref[...], preferred_element_type=jnp.float32)
            if adds:
                block = block + refs[0][slot].astype(jnp.float32)
            out_ref[slot] = block.astype(out_ref.dtype)

    if len(out_refs) == 1:
        write(out_refs[0])
        return
    for step, out_ref in enumerate(out_refs):
        pl.when(pl.program_id(0) == step)(functools.partial(write, out_ref))


def grad_blocks(tokens, turned, row, new_owner, first, steps, per_step, addend=None, cut=False):
    rows, features = tokens.shape
    width = turned.shape[0]
    blocks = steps * per_step
    groups = lax.axis_size("rep")
    row_block = features // (groups * new_owner.shape[0])
    if row_block % 128:
        chosen = row[first : first + blocks]
        chosen = jnp.take(new_owner, chosen % new_owner.shape[0]) * groups + (
            chosen // new_owner.shape[0]
        )
        whole = jnp.dot(turned, tokens, preferred_element_type=jnp.float32)
        parts = jnp.transpose(whole.reshape(width, features // row_block, row_block), (1, 0, 2))
        parts = jnp.take(parts, chosen, axis=0)
        if addend is not None:
            parts = parts + addend.astype(jnp.float32)
        parts = parts.astype(jnp.bfloat16)
        return list(jnp.split(parts, steps)) if cut else [parts]

    def token_map(slot):
        return lambda i, row_ref, new_ref: (
            0,
            block_at(new_ref, groups, row_ref[first + i * per_step + slot]),
        )

    block = pl.BlockSpec((per_step, width, row_block), lambda i, *_: (i, 0, 0))
    fixed = pl.BlockSpec((per_step, width, row_block), lambda i, *_: (0, 0, 0))
    added = [] if addend is None else [addend]
    outs = steps if cut else 1
    return pl.pallas_call(
        functools.partial(grad_kernel, per_step, len(added)),
        grid_spec=pltpu.PrefetchScalarGridSpec(
            num_scalar_prefetch=2,
            grid=(steps,),
            in_specs=[pl.BlockSpec((rows, row_block), token_map(s)) for s in range(per_step)]
            + [pl.BlockSpec((width, rows), lambda i, *_: (0, 0))]
            + [block] * len(added),
            out_specs=[fixed if cut else block] * outs,
        ),
        out_shape=[jax.ShapeDtypeStruct((blocks // outs, width, row_block), jnp.bfloat16)] * outs,
        compiler_params=pltpu.CompilerParams(vmem_limit_bytes=GRANT),
        cost_estimate=cost(
            2 * rows * width * blocks * row_block,
            2 * blocks * row_block * (rows + width * (1 + len(added))) + 2 * rows * width,
        ),
        name="weight_gradient",
    )(row, new_owner, *([tokens] * per_step), turned, *added)


def pack_kernel(groups, new_ref, first_ref, second_ref, out_ref):
    for slot in range(out_ref.shape[0]):
        block = block_at(new_ref, groups, slot)
        rows = pl.ds(pl.multiple_of(block * SUB, SUB), SUB)
        pair = jnp.concatenate([first_ref[rows, :], second_ref[rows, :]], axis=0)
        out_ref[slot] = pair.astype(out_ref.dtype)


def pack_moments(first, second, new_owner, groups):
    devices = new_owner.shape[0] * groups
    width = first.shape[1]
    return pl.pallas_call(
        functools.partial(pack_kernel, groups),
        in_specs=[
            pl.BlockSpec(memory_space=pltpu.SMEM),
            pl.BlockSpec(memory_space=pltpu.VMEM),
            pl.BlockSpec(memory_space=pltpu.VMEM),
        ],
        out_specs=pl.BlockSpec(memory_space=pltpu.VMEM),
        out_shape=jax.ShapeDtypeStruct((devices, 2 * SUB, width), jnp.bfloat16),
        cost_estimate=cost(0, 12 * first.size),
        name="pack_moments",
    )(new_owner, first, second)


def project_kernel(groups, first, own, row_ref, old_ref, new_ref, token_ref, *refs):
    piece_refs, (out_ref, rows_ref, held, logical, sems) = refs[:-5], refs[-5:]
    devices, row_block, _ = held.shape

    @pl.when(pl.program_id(0) == 0)
    def _():
        copies = []
        for piece_ref in piece_refs:
            for index in range(piece_ref.shape[0]):
                slot = len(copies)
                target = held.at[old_ref[row_ref[first + slot]]]
                copies.append(pltpu.make_async_copy(piece_ref.at[index], target, sems.at[slot]))
        for copy in copies:
            copy.start()
        for copy in copies:
            copy.wait()

        def place(pair, carry):
            for block in range(0, devices, 2):
                span = pl.ds(block * SUB, 2 * SUB)
                top = held[2 * pair, span, :]
                low = held[2 * pair + 1, span, :]
                for half in range(2):
                    part = slice(half * SUB, (half + 1) * SUB)
                    start = (block + half) * row_block + pair * 2 * SUB
                    logical[pl.ds(pl.multiple_of(start, 2 * SUB), 2 * SUB), :] = jnp.concatenate(
                        [top[part], low[part]], axis=0
                    )
            return carry

        lax.fori_loop(0, devices // 2, place, 0)
        start = block_at(new_ref, groups, row_ref[own]) * row_block
        start = pl.multiple_of(start, row_block)
        rows_ref[...] = logical[pl.ds(start, row_block), :]

    out_ref[...] = jnp.dot(
        token_ref[...], logical[...], preferred_element_type=jnp.float32
    ).astype(out_ref.dtype)


def project(tokens, pieces, row, first, own, old_owner, new_owner):
    rows, features = tokens.shape
    _, row_block, width = pieces[0].shape
    devices = old_owner.shape[0]
    tile = rows // 4
    return pl.pallas_call(
        functools.partial(project_kernel, devices // new_owner.shape[0], first, own),
        grid_spec=pltpu.PrefetchScalarGridSpec(
            num_scalar_prefetch=3,
            grid=(rows // tile,),
            in_specs=[pl.BlockSpec((tile, features), lambda i, *_: (i, 0))]
            + [pl.BlockSpec(memory_space=pl.ANY)] * len(pieces),
            out_specs=[
                pl.BlockSpec((tile, width), lambda i, *_: (i, 0)),
                pl.BlockSpec((row_block, width), lambda i, *_: (0, 0)),
            ],
            scratch_shapes=[
                pltpu.VMEM((devices, row_block, width), jnp.bfloat16),
                pltpu.VMEM((features, width), jnp.bfloat16),
                pltpu.SemaphoreType.DMA((devices,)),
            ],
        ),
        out_shape=[
            jax.ShapeDtypeStruct((rows, width), jnp.bfloat16),
            jax.ShapeDtypeStruct((row_block, width), jnp.bfloat16),
        ],
        compiler_params=pltpu.CompilerParams(vmem_limit_bytes=GRANT),
        cost_estimate=cost(
            2 * rows * width * features, 2 * (rows * features + features * width + rows * width)
        ),
        name="project",
    )(row, old_owner, new_owner, tokens, *pieces)


def adam(weight_rows, first_rows, second_rows, gradient):
    first_next = beta_one * first_rows + (1.0 - beta_one) * gradient
    second_next = beta_two * second_rows + (1.0 - beta_two) * gradient * gradient
    step_size = first_next / correction_one / (jnp.sqrt(second_next / correction_two) + epsilon)
    updated = (
        weight_rows.astype(jnp.float32) * (1.0 - learn_rate * decay_rate) - learn_rate * step_size
    ).astype(jnp.bfloat16)
    return updated, first_next, second_next


def adam_kernel(owner_ref, moments_ref, weight_ref, *refs):
    part_refs, (new_ref, first_ref, second_ref, gradient, inverse_ref) = refs[:-5], refs[-5:]
    for slot in range(moments_ref.shape[0]):
        inverse_ref[owner_ref[slot]] = slot
    total = part_refs[0][0].astype(jnp.float32)
    for part_ref in part_refs[1:]:
        total = total + part_ref[0].astype(jnp.float32)
    gradient[...] = total.T
    for pair in range(moments_ref.shape[0] // 2):
        even = moments_ref[inverse_ref[2 * pair]].astype(jnp.float32)
        odd = moments_ref[inverse_ref[2 * pair + 1]].astype(jnp.float32)
        rows = pl.ds(pair * 2 * SUB, 2 * SUB)
        new_ref[rows, :], first_ref[rows, :], second_ref[rows, :] = adam(
            weight_ref[rows, :],
            jnp.concatenate([even[:SUB], odd[:SUB]], axis=0),
            jnp.concatenate([even[SUB:], odd[SUB:]], axis=0),
            gradient[rows, :],
        )


def adam_rows(parts, moments, weight_rows, owners):
    row_block, width = weight_rows.shape
    whole = pl.BlockSpec((row_block, width), lambda i, *_: (0, 0))
    return pl.pallas_call(
        adam_kernel,
        grid_spec=pltpu.PrefetchScalarGridSpec(
            num_scalar_prefetch=1,
            grid=(1,),
            in_specs=[pl.BlockSpec(moments.shape, lambda i, *_: (0, 0, 0)), whole]
            + [pl.BlockSpec((1, width, row_block), lambda i, *_: (0, 0, 0))] * len(parts),
            out_specs=[whole] * 3,
            scratch_shapes=[
                pltpu.VMEM((row_block, width), jnp.float32),
                pltpu.SMEM((moments.shape[0],), jnp.int32),
            ],
        ),
        out_shape=[
            jax.ShapeDtypeStruct((row_block, width), jnp.bfloat16),
            jax.ShapeDtypeStruct((row_block, width), jnp.float32),
            jax.ShapeDtypeStruct((row_block, width), jnp.float32),
        ],
        compiler_params=pltpu.CompilerParams(vmem_limit_bytes=GRANT),
        cost_estimate=cost(20 * row_block * width, 16 * row_block * width),
        name="adam_rows",
    )(owners, moments, weight_rows, *parts)


class Grid:
    def __init__(self, groups, shards):
        self.shards = shards
        self.cores = 2 if groups % 2 == 0 else 1
        self.minor = 2 if shards % 2 == 0 else 1
        self.outer = groups // self.cores
        self.far = shards // self.minor
        self.swaps = self.cores == 2 and self.minor == self.outer
        self.near, self.side = self.minor, self.outer

    def moved(self, position, core=0, near=0, side=0, far=0):
        group, shard = position // self.shards, position % self.shards
        outer, on = group // self.cores, (group % self.cores + core) % self.cores
        depth, minor = shard // self.minor, shard % self.minor
        swapped = on if self.swaps else 0
        minor = (minor + near + (side - near) * swapped) % self.minor
        outer = (outer + side + (near - side) * swapped) % self.outer
        depth = (depth + far) % self.far
        return (outer * self.cores + on) * self.shards + depth * self.minor + minor

    def send(self, value, **steps):
        devices = self.outer * self.cores * self.shards
        pairs = [(p, self.moved(p, **steps)) for p in range(devices)]
        return lax.ppermute(value, AXES, pairs)


def rounded_sum(*terms):
    total = terms[0].astype(jnp.float32)
    for term in terms[1:]:
        total = total + term.astype(jnp.float32)
    return total.astype(terms[0].dtype)


def chunks(grid):
    half = grid.far // 2
    return [sorted({d, (grid.far - d) % grid.far}) for d in range(half + 1)]


def tables(grid, devices):
    sums = [
        dict(core=core, near=near, side=side, far=far)
        for chunk in chunks(grid)
        for core in range(grid.cores)
        for near in [*range(1, grid.near), 0]
        for side in range(grid.side)
        for far in chunk
    ]
    shards = [
        dict(core=-core, near=-near, side=-side, far=-far)
        for chunk in chunks(grid)
        for core in range(grid.cores)
        for near in range(grid.near)
        for side in range(grid.side)
        for far in chunk
    ]
    return np.array(
        [[grid.moved(p, **step) for step in sums + shards] for p in range(devices)], np.int32
    )


def reduce_rows(grid, blocks_of):
    last = []
    start = grid.far
    for chunk in reversed(chunks(grid)):
        count = len(chunk)
        start -= count
        addend = None
        if grid.cores > 1:
            addend = grid.send(blocks_of(1, start, count, None, False)[0], core=1)
        parts = blocks_of(0, start, count, addend, True)
        kept = [parts[-1]]
        for step, part in enumerate(parts[:-1], 1):
            kept.append(grid.send(part, near=step))
        ends = list(kept)
        for step in range(1, grid.side):
            cut = slice(step * count, (step + 1) * count)
            ends.append(grid.send(rounded_sum(*[t[cut] for t in kept]), side=step))
        if chunk == [0]:
            last.extend(ends)
            continue
        for index, far in enumerate(chunk):
            cut = slice(index, index + 1)
            last.append(grid.send(rounded_sum(*[t[cut] for t in ends]), far=far))
    return last


def gather_shards(grid, own):
    arrived = {far: grid.send(own, far=far) for far in range(1, grid.far)}
    arrived[0] = own
    pieces = []
    for chunk in chunks(grid):
        base = joined([arrived[far] for far in chunk])
        plane = joined([base] + [grid.send(base, side=step) for step in range(1, grid.side)])
        both = [plane] + [grid.send(plane, near=step) for step in range(1, grid.near)]
        pieces += both
        for core in range(1, grid.cores):
            pieces += [grid.send(part, core=core) for part in both]
    return pieces


def joined(arrays):
    return arrays[0] if len(arrays) == 1 else jnp.concatenate(arrays, axis=0)


def body(tokens, cotangent, old_weight, old_first, old_second, old_owner, new_owner):
    devices = lax.axis_size(AXES)
    groups = lax.axis_size("rep")
    shards = lax.axis_size("fsdp")
    features = tokens.shape[1]
    row_block, width = old_weight.shape
    strip = row_block * width // devices
    grid = Grid(groups, shards)
    me = lax.axis_index(AXES)
    by_tile = row_block == devices * SUB and width % 128 == 0 and devices % 2 == 0

    row = lax.dynamic_index_in_dim(jnp.asarray(tables(grid, devices)), me, 0, keepdims=False)
    per_far = grid.near * grid.side
    own = (grid.near - 1) * grid.side

    pieces = gather_shards(grid, old_weight[None])
    if by_tile:
        packed = pack_moments(old_first, old_second, new_owner, groups)
    else:
        slot_ids = jnp.arange(devices, dtype=jnp.int32)
        placing = jnp.take(new_owner, slot_ids % shards) * groups + slot_ids // shards
        both = jnp.stack([old_first, old_second]).astype(jnp.bfloat16)
        packed = jnp.take(
            jnp.transpose(both.reshape(2, devices, strip), (1, 0, 2)), placing, axis=0
        )
    arrived = lax.all_to_all(packed, AXES, split_axis=0, concat_axis=0, tiled=True)

    turned = cotangent.T

    def blocks_of(core, start, count, addend, cut):
        first = (start * grid.cores + core * count) * per_far
        per_step = grid.side * count
        return grad_blocks(
            tokens, turned, row, new_owner, first, grid.near, per_step, addend, cut
        )

    parts = reduce_rows(grid, blocks_of)
    if by_tile:
        projected, weight_rows = project(tokens, pieces, row, devices, own, old_owner, new_owner)
        return (projected, *adam_rows(parts, arrived, weight_rows, old_owner))
    inverse = jnp.zeros((devices,), jnp.int32).at[old_owner].set(slot_ids)
    held = jnp.zeros((devices, devices, strip), jnp.bfloat16)
    held = held.at[jnp.take(old_owner, row[devices:])].set(
        joined(pieces).reshape(devices, devices, strip)
    )
    logical = jnp.transpose(held, (1, 0, 2)).reshape(features, width)
    projected = jnp.dot(tokens, logical, preferred_element_type=jnp.float32).astype(jnp.bfloat16)
    own_block = jnp.take(placing, me)
    weight_rows = lax.dynamic_slice_in_dim(logical, own_block * row_block, row_block, 0)
    moved = jnp.transpose(jnp.take(arrived, inverse, axis=0), (1, 0, 2))
    first_rows, second_rows = moved.astype(jnp.float32).reshape(2, row_block, width)
    gradient = sum(part[0].astype(jnp.float32) for part in parts).T
    return (projected, *adam(weight_rows, first_rows, second_rows, gradient))


def solution(mesh):
    placed = P(AXES, None)
    return jax.shard_map(
        body,
        mesh=mesh,
        in_specs=(placed,) * 5 + (P(), P()),
        out_specs=(placed,) * 4,
        check_vma=False,
    )
```
